512 devices in a mesh: grp: 16 (over x, z_hi, core), ctx: 32 (over y, z_lo).
Axes of the slice: x: 4, y: 8, z: 8 (z_hi: 2, z_lo: 4; z = z_hi * 4 + z_lo), core: 2. Of those that a mesh axis runs over, the one named last changes fastest.
Arguments:
- queries: bfloat16 [8192, 4096], P('ctx', 'grp'), may hold values from -4 to 4
- keys: bfloat16 [8192, 512], P('ctx'), may hold values from -4 to 4
- values: bfloat16 [8192, 512], P('ctx'), may hold values from -6 to 6
- attn_gate: bfloat16 [8192, 4096], P('ctx', 'grp'), may hold values from -6 to 6
- delta_query: bfloat16 [8192, 2048], P('ctx', 'grp'), may hold values from -6 to 6
- delta_key: bfloat16 [8192, 2048], P('ctx', 'grp'), may hold values from -6 to 6
- delta_value: bfloat16 [8192, 4096], P('ctx', 'grp'), may hold values from -6 to 6
- delta_gate: bfloat16 [8192, 4096], P('ctx', 'grp'), may hold values from -6 to 6
- decay_log: float32 [32, 8192], P('grp', 'ctx'), may hold values from -0.7 to 0
- beta: float32 [32, 8192], P('grp', 'ctx'), may hold values from 0.005 to 0.9
- norm_gain: float32 [128], replicated, may hold values from 0.1 to 1.9
- attn_out_weight: bfloat16 [4096, 2048], P('grp'), may hold values from -0.125 to 0.125
- delta_out_weight: bfloat16 [4096, 2048], P('grp'), may hold values from -0.125 to 0.125
- doc_lengths: int32 [4], replicated, may hold values from 1 to 64, 128 in all
Outputs:
- attn_mixed: bfloat16 [8192, 2048], P('ctx', 'grp')
- delta_mixed: bfloat16 [8192, 2048], P('ctx', 'grp')
The draws below stay inside these ranges and needn't reach their ends.
Inputs may be any that keep to these rules, and one draw needn't show every extreme that they name: `doc_lengths`: lengths of the 4 prompts in order along the sequence, counted in blocks of 64 tokens; they cover the whole sequence and the longest covers exactly half of its blocks.
All inputs are finite; a program needn't handle non-finite values.
Results may differ from the reference program's by a relative error of at most 0.023.
Values may be sent and summed in bfloat16 or wider, within the bound.
A program may use at most 64 MiB of HBM per device.

```python
import math
import jax
import jax.numpy as jnp
import numpy as np
from jax import lax

D = 2048
HEADS = 16
HD = 256
KVH = 2
VALUE_HEADS = 32
KH = 16
DHD = 128
BLOCK = 64
DOCS = 4
TOKEN_COUNT = 8192
N_GRP = 16


def head_blend(key):
    key_category, key_spike = jax.random.split(key, 2)
    head_category = jax.random.uniform(key_category, (VALUE_HEADS, 1), jnp.float32)
    spike_mask = jax.random.randint(key_spike, (VALUE_HEADS, TOKEN_COUNT), 0, 4096) == 0
    return (head_category, spike_mask)


def draw_queries(key, part):
    key = jax.random.fold_in(key, 11)
    base_draw = jax.random.normal(key, (TOKEN_COUNT, HEADS * HD), jnp.float32)
    return jnp.clip(base_draw, -4.0, 4.0).astype(jnp.bfloat16)


def draw_keys(key, part):
    key = jax.random.fold_in(key, 12)
    base_draw = jax.random.normal(key, (TOKEN_COUNT, KVH * HD), jnp.float32)
    return jnp.clip(base_draw, -4.0, 4.0).astype(jnp.bfloat16)


def draw_decay_log(key, part):
    head_category, spike_mask = head_blend(key)
    key = jax.random.fold_in(key, 21)
    key_slow, key_fast, key_dropout = jax.random.split(key, 3)
    slow_share = 0.5
    slow_heads = head_category < slow_share
    gradual_rate = jnp.exp(jax.random.uniform(key_slow, (VALUE_HEADS, TOKEN_COUNT), jnp.float32, math.log(1e-05), math.log(4e-05)))
    fast_rate = jnp.exp(jax.random.uniform(key_fast, (VALUE_HEADS, TOKEN_COUNT), jnp.float32, math.log(1.0 / 50.0), math.log(1.0 / 30.0)))
    spike_drop_level = jax.random.uniform(key_dropout, (VALUE_HEADS, TOKEN_COUNT), jnp.float32, math.log(0.5), math.log(0.8))
    gradual_value = jnp.where(spike_mask, spike_drop_level, -gradual_rate)
    return jnp.where(slow_heads, gradual_value, -fast_rate).astype(jnp.float32)


def draw_beta(key, part):
    head_category, spike_mask = head_blend(key)
    key = jax.random.fold_in(key, 22)
    key_slow, key_fast = jax.random.split(key, 2)
    slow_share = 0.5
    slow_heads = head_category < slow_share
    slow_write = jnp.exp(jax.random.uniform(key_slow, (VALUE_HEADS, TOKEN_COUNT), jnp.float32, math.log(0.005), math.log(0.05)))
    fast_write = jax.random.uniform(key_fast, (VALUE_HEADS, TOKEN_COUNT), jnp.float32, 0.2, 0.9)
    return jnp.where(slow_heads, slow_write, fast_write).astype(jnp.float32)


def raised(values, key, source, target, parts, factor):
    owner, partner = [(jnp.arange(values.shape[dim]) // (values.shape[dim] // parts)).reshape([-1 if axis == dim else 1 for axis in range(values.ndim)]) for dim in (source, target)]
    chosen = jax.random.permutation(key, parts)[partner]
    strong = (owner == chosen) | (owner == (partner + parts // 2) % parts)
    return jnp.where(strong, factor * values, values)


def steps_of(key, extent, shards, smallest, high):
    level = 1.0
    for dim, parts in shards:
        draws = jax.random.uniform(jax.random.fold_in(jax.random.fold_in(key, 6), dim), (parts,), jnp.float32, smallest / len(shards), high / len(shards))
        level = level * jnp.repeat(jnp.exp(draws), extent[dim] // parts).reshape((-1,) + (1,) * (len(extent) - 1 - dim))
    return level


def length_profile(amount, total, bound, slope):
    weights = [(1 << 20) // math.isqrt(rank ** slope) + 1 for rank in range(2, amount + 1)]
    rest, holding = total - bound - (amount - 1), [1] * (amount - 1)
    while rest > 0:
        free = [i for i in range(amount - 1) if holding[i] < bound]
        pool, budget = sum([weights[i] for i in free]), rest
        for i in free:
            extra = min(bound - holding[i], max(1, budget * weights[i] // pool), rest)
            holding[i] = holding[i] + extra
            rest = rest - extra
    return np.array([bound] + holding)


def uneven(stream_key, count, total, most, lean):
    if count == 2:
        one = jax.random.randint(stream_key, (), max(1, total - most), min(most, total - 1) + 1)
        return jnp.stack([one, total - one])
    tallies = jnp.asarray(length_profile(count, total, most, lean), jnp.int32)
    pairs = (count - 1) // 2
    source_of, taker = tallies[1:1 + 2 * pairs:2], tallies[2:2 + 2 * pairs:2]
    slack = jnp.minimum(source_of - 1, most - taker)
    passed = jax.random.randint(jax.random.fold_in(stream_key, 1), (pairs,), 0, 1 << 20) % (slack + 1)
    tallies = tallies.at[1:1 + 2 * pairs:2].set(source_of - passed).at[2:2 + 2 * pairs:2].set(taker + passed)
    return tallies[jax.random.permutation(jax.random.fold_in(stream_key, 2), count)]


def noise(rng, shape, spread, bound, pieces=(), kind=jnp.bfloat16):
    values = jax.random.normal(rng, shape, jnp.float32) * spread
    if len(pieces) > 0:
        values = steps_of(rng, shape, pieces, -0.22, 0.18) * values
    return jnp.clip(values, min=-bound, max=bound).astype(kind)


def gaussian_with(own_key, dims, width, limit, cuts, heavy, held_as=jnp.bfloat16):
    values = width * jax.random.normal(own_key, dims, jnp.float32)
    if cuts:
        values = values * steps_of(own_key, dims, cuts, -0.22, 0.18)
    return jnp.clip(raised(values, jax.random.fold_in(own_key, 3), *heavy), -limit, limit).astype(held_as)


def setup_inputs(seed: int = 0) -> dict:
    arg_keys = jax.random.split(jax.random.key(seed), 15)
    return {
        "queries": draw_queries(jax.random.fold_in(arg_keys[14], 71), 0),
        "keys": draw_keys(jax.random.fold_in(arg_keys[14], 71), 0),
        "values": noise(arg_keys[2], (TOKEN_COUNT, KVH * HD), 1.0, 6.0, ((0, 32),)),
        "attn_gate": noise(arg_keys[3], (TOKEN_COUNT, HEADS * HD), 1.0, 6.0, ((0, 32), (1, 16))),
        "delta_query": noise(arg_keys[4], (TOKEN_COUNT, KH * DHD), 1.0, 6.0, ((0, 32), (1, 16))),
        "delta_key": noise(arg_keys[5], (TOKEN_COUNT, KH * DHD), 1.0, 6.0, ((0, 32), (1, 16))),
        "delta_value": noise(arg_keys[6], (TOKEN_COUNT, VALUE_HEADS * DHD), 1.0, 6.0, ((0, 32), (1, 16))),
        "delta_gate": noise(arg_keys[7], (TOKEN_COUNT, VALUE_HEADS * DHD), 1.0, 6.0, ((0, 32), (1, 16))),
        "decay_log": draw_decay_log(jax.random.fold_in(arg_keys[14], 71), 0),
        "beta": draw_beta(jax.random.fold_in(arg_keys[14], 71), 0),
        "norm_gain": jnp.clip(1.0 + 0.18 * jax.random.normal(arg_keys[10], (DHD,), jnp.float32), 0.1, 1.9),
        "attn_out_weight": gaussian_with(arg_keys[11], (HEADS * HD, D), (HEADS * HD) ** -0.5, 0.125, ((0, 16),), (0, 1, 16, 2.0)),
        "delta_out_weight": gaussian_with(arg_keys[12], (VALUE_HEADS * DHD, D), (VALUE_HEADS * DHD) ** -0.5, 0.125, ((0, 16),), (0, 1, 16, 2.0)),
        "doc_lengths": uneven(arg_keys[13], DOCS, TOKEN_COUNT // BLOCK, TOKEN_COUNT // BLOCK // 2, 2).astype(jnp.int32),
    }


epsilon = 1e-06
masked_score = -1e+30
highest = lax.Precision.HIGHEST

def prompt_index(positions, prompt_ends):
    return lax.optimization_barrier(jnp.sum((positions[:, None] >= prompt_ends[None, :]).astype(jnp.int32), axis=1))

def gated_norm(core_out, gate_input, norm_gain):
    squares = lax.optimization_barrier(jnp.mean(core_out * core_out, axis=-1, keepdims=True))
    normed = core_out * lax.rsqrt(squares + epsilon) * norm_gain.astype(jnp.float32)
    gate_value = gate_input.astype(jnp.float32).reshape(core_out.shape)
    gated = (normed * jax.nn.silu(gate_value)).astype(jnp.bfloat16)
    return gated.reshape(core_out.shape[0], core_out.shape[1] * core_out.shape[2])

def unit_heads(inputs, head_count):
    shaped = inputs.astype(jnp.float32).reshape(inputs.shape[0], head_count, DHD)
    return shaped * lax.rsqrt(lax.optimization_barrier(jnp.sum(shaped * shaped, axis=-1, keepdims=True)) + epsilon)

def attention_heads(queries, keys, values, attn_gate, prompt_ends):
    query_block = math.gcd(TOKEN_COUNT, 512)
    positions = jnp.arange(TOKEN_COUNT, dtype=jnp.int32)
    prompt_of = prompt_index(positions, prompt_ends)
    group_size = HEADS // KVH
    score_scale = HD ** (-0.5)

    def head_output(head_at):
        head_queries = lax.dynamic_slice_in_dim(queries, head_at * HD, HD, 1)
        kv_head = head_at // group_size
        head_keys = lax.dynamic_slice_in_dim(keys, kv_head * HD, HD, 1)
        head_values = lax.dynamic_slice_in_dim(values, kv_head * HD, HD, 1)

        def block_output(block_at):
            first_row = block_at * query_block
            block_queries = lax.dynamic_slice_in_dim(head_queries, first_row, query_block, 0)
            block_pos = first_row + jnp.arange(query_block, dtype=jnp.int32)
            block_prompt = lax.dynamic_slice_in_dim(prompt_of, first_row, query_block, 0)
            scores = lax.dot_general(block_queries, head_keys, (((1,), (1,)), ((), ())), preferred_element_type=jnp.float32) * score_scale
            allowed = (positions[None, :] <= block_pos[:, None]) & (prompt_of[None, :] == block_prompt[:, None])
            scores = jnp.where(allowed, scores, masked_score)
            row_max = lax.optimization_barrier(jnp.max(scores, axis=1, keepdims=True))
            weights = jnp.where(allowed, jnp.exp(scores - row_max), 0.0)
            totals = lax.optimization_barrier(jnp.sum(weights, axis=1, keepdims=True))
            return jnp.dot(weights.astype(jnp.bfloat16), head_values, preferred_element_type=jnp.float32) / totals
        blocks = lax.map(block_output, jnp.arange(TOKEN_COUNT // query_block, dtype=jnp.int32))
        return blocks.reshape(TOKEN_COUNT, HD)
    per_head = lax.map(head_output, jnp.arange(HEADS, dtype=jnp.int32))
    core_out = per_head.transpose(1, 0, 2).reshape(TOKEN_COUNT, HEADS * HD)
    return (core_out * jax.nn.sigmoid(attn_gate.astype(jnp.float32))).astype(jnp.bfloat16)

def deltanet_heads(delta_query, delta_key, delta_value, delta_gate, decay_log, beta, norm_gain, doc_lengths):
    share_ratio = VALUE_HEADS // KH
    query_unit = jnp.repeat(unit_heads(delta_query, KH), share_ratio, axis=1)
    key_unit = jnp.repeat(unit_heads(delta_key, KH), share_ratio, axis=1)
    value_rows = delta_value.astype(jnp.float32).reshape(TOKEN_COUNT, VALUE_HEADS, DHD)
    lengths = doc_lengths.astype(jnp.int32)
    prompt_starts = ((jnp.cumsum(lengths) - lengths) * BLOCK).astype(jnp.int32)
    positions = jnp.arange(TOKEN_COUNT, dtype=jnp.int32)
    keep_token = 1.0 - jnp.any(positions[:, None] == prompt_starts[None, :], axis=1).astype(jnp.float32)
    factors = jnp.exp(decay_log).T
    strengths = beta.T

    def advance(carried, entries):
        query_now, key_now, value_now, factor_now, strength_now, keep_now = entries
        carried = carried * (keep_now * factor_now)[:, None, None]
        recalled = jnp.einsum('hd,hde->he', key_now, carried, precision=highest)
        carried = carried + strength_now[:, None, None] * key_now[:, :, None] * (value_now - recalled)[:, None, :]
        return (carried, jnp.einsum('hd,hde->he', query_now, carried, precision=highest))
    start_state = jnp.zeros((VALUE_HEADS, DHD, DHD), jnp.float32)
    _, core_out = lax.scan(advance, start_state, (query_unit, key_unit, value_rows, factors, strengths, keep_token))
    return gated_norm(core_out, delta_gate, norm_gain)

def project_rows(heads, weight):
    group_width = heads.shape[1] // N_GRP

    def add_group(summed, group_at):
        part_heads = lax.dynamic_slice_in_dim(heads, group_at * group_width, group_width, 1)
        part_weight = lax.dynamic_slice_in_dim(weight, group_at * group_width, group_width, 0)
        group_term = jnp.dot(part_heads, part_weight, preferred_element_type=jnp.float32).astype(jnp.bfloat16)
        group_term = lax.optimization_barrier(group_term).astype(jnp.float32)
        return (summed + group_term, None)
    summed, _ = lax.scan(add_group, jnp.zeros((TOKEN_COUNT, D), jnp.float32), jnp.arange(N_GRP, dtype=jnp.int32))
    return summed.astype(jnp.bfloat16)

def reference(queries, keys, values, attn_gate, delta_query, delta_key, delta_value, delta_gate, decay_log, beta, norm_gain, attn_out_weight, delta_out_weight, doc_lengths):
    prompt_ends = (jnp.cumsum(doc_lengths.astype(jnp.int32)) * BLOCK).astype(jnp.int32)
    attn_heads = attention_heads(queries, keys, values, attn_gate, prompt_ends)
    delta_heads = deltanet_heads(delta_query, delta_key, delta_value, delta_gate, decay_log, beta, norm_gain, doc_lengths)
    return (project_rows(attn_heads, attn_out_weight), project_rows(delta_heads, delta_out_weight))
```

```python
import functools

import jax
import jax.numpy as jnp
from jax import lax
from jax.experimental import pallas as pl
from jax.experimental.pallas import tpu as pltpu
from jax.sharding import PartitionSpec as P

MESH = pl.DeviceIdType.MESH
F32 = jnp.float32
BF16 = jnp.bfloat16

HEADS = 16
HD = 256
KVH = 2
DHD = 128
BLOCK = 64
TOK = 256
PIECE = 64
MSG = 2 * DHD + 16

EPS = 1e-06
MASKED = -2e30
START_MAX = -1e30

NT = (((1,), (1,)), ((), ()))
NN = (((1,), (0,)), ((), ()))


def dot(a, b, dims=NN):
    return lax.dot_general(a, b, dims, preferred_element_type=F32)


def split(x):
    high = x.astype(BF16)
    return high, (x - high.astype(F32)).astype(BF16)


def dot3(a, b):
    ah, al = a
    bh, bl = b
    return dot(ah, bh) + (dot(ah, bl) + dot(al, bh))


def dot2(a, b):
    return dot(a[0], b) + dot(a[1], b)


def kernel(
    ends_ref,
    q_ref,
    k_ref,
    v_ref,
    agate_ref,
    dq_ref,
    dk_ref,
    dv_ref,
    dgate_ref,
    decay_ref,
    beta_ref,
    gain_ref,
    wa_hbm,
    wd_hbm,
    oa_ref,
    od_ref,
    wa_ref,
    wd_ref,
    qall,
    kv,
    bias,
    acc,
    stat,
    accs,
    accr,
    stats,
    statr,
    own,
    csend,
    crecv,
    eff,
    pbuf,
    r1,
    s2,
    r2,
    s3,
    r3,
    w_sem,
    q_s,
    q_r,
    z_s,
    y_s,
    kv_r,
    c_s,
    c_r,
    a_s,
    a_r,
    t_s,
    t_r,
    s1_s,
    s1_r,
    s2_s,
    s2_r,
    s3_s,
    s3_r,
):
    grp = lax.axis_index("grp")
    ctx = lax.axis_index("ctx")
    x, zh, c = grp // 4, (grp // 2) % 2, grp % 2
    y, z = ctx // 4, ctx % 4
    xb = x % 2
    kvh = x // 2
    member = xb * 2 + c

    def grp_of(x_, zh_, c_):
        return x_ * 4 + zh_ * 2 + c_

    xn = x + 1 - 2 * xb
    quad = [(x, 1 - c), (xn, c), (xn, 1 - c)]
    quad_grp = [grp_of(a, zh, b) for a, b in quad]
    quad_member = [(a % 2) * 2 + b for a, b in quad]
    x_grp = [grp_of((x + d) % 4, zh, c) for d in (1, 2, 3)]
    z_grp = grp_of(x, 1 - zh, c)
    sib_grp = quad_grp[0]
    row_ctx = [y * 4 + (z + d) % 4 for d in (1, 2, 3)]

    def copy(src, dst, send, recv, g, r):
        return pltpu.make_async_remote_copy(
            src_ref=src,
            dst_ref=dst,
            send_sem=send,
            recv_sem=recv,
            device_id={"grp": g, "ctx": r},
            device_id_type=MESH,
        )

    def arrived(dst, sem):
        pltpu.make_async_copy(dst, dst, sem).wait()

    sends = []

    barrier = pltpu.get_barrier_semaphore()
    peers = [(g, ctx) for g in quad_grp + x_grp + [z_grp]]
    peers += [(grp, r) for r in row_ctx]
    peers += [(grp, (ctx + d) % 32) for d in (1, 31, 2, 30, 4, 28, 8, 24)]
    for g, r in peers:
        pl.semaphore_signal(barrier, inc=1, device_id={"grp": g, "ctx": r}, device_id_type=MESH)

    wa_copy = pltpu.make_async_copy(wa_hbm, wa_ref, w_sem.at[0])
    wd_copy = pltpu.make_async_copy(wd_hbm, wd_ref, w_sem.at[1])
    wa_copy.start()
    wd_copy.start()

    rows = pl.ds(pl.multiple_of(member * PIECE, PIECE), PIECE)
    cols = pl.ds(pl.multiple_of(kvh * HD, HD), HD)
    kv[0, 0, z] = k_ref[rows, cols]
    kv[0, 1, z] = v_ref[rows, cols]
    qall[member] = q_ref[...] * jnp.asarray(HD ** (-0.5), BF16)
    pl.semaphore_wait(barrier, len(peers))

    def forward(dy, zs):
        return copy(
            kv.at[dy, :, zs], kv.at[dy + 1, :, zs], y_s.at[dy * 4 + zs], kv_r.at[dy * 4 + 4 + zs], grp, ctx + 4
        )

    @pl.when(y < 7)
    def _():
        forward(0, z).start()

    for i in range(3):
        copy(kv.at[0, :, z], kv.at[0, :, z], z_s.at[i], kv_r.at[z], grp, row_ctx[i]).start()
    for i in (1, 2, 0):
        copy(qall.at[member], qall.at[member], q_s.at[i], q_r.at[i], quad_grp[i], ctx).start()

    ticks = [(dy, i) for dy in range(5) for i in range(4)][1:]

    def tick(count=1):
        for _ in range(count):
            if not ticks:
                return
            dy, i = ticks.pop(0)
            zs = (z + i) % 4

            @pl.when(y >= dy)
            def _():
                arrived(kv.at[dy, :, zs], kv_r.at[dy * 4 + zs])

                if dy < 4:

                    @pl.when(y < 7)
                    def _():
                        forward(dy, zs).start()

    def tick_through(dy):
        while ticks and ticks[0][0] <= dy:
            tick()

    first = ctx * TOK
    ends = [ends_ref[i] for i in range(4)]

    def prompt(pos):
        total = (pos >= ends[0]).astype(F32)
        for e in ends[1:]:
            total += (pos >= e).astype(F32)
        return total

    row_i = lax.broadcasted_iota(jnp.int32, (1, TOK), 1)
    col_i = lax.broadcasted_iota(jnp.int32, (TOK, 1), 0)
    pid_row = prompt(first + row_i)
    pid_col = prompt(first + col_i)
    pid_before = prompt(jnp.full((1, 1), first - 1, jnp.int32))
    pid_last = prompt(jnp.full((1, 1), first + TOK - 1, jnp.int32))

    ii = lax.broadcasted_iota(jnp.int32, (TOK, TOK), 0)
    jj = lax.broadcasted_iota(jnp.int32, (TOK, TOK), 1)
    lower = (jj <= ii) & (pid_col == pid_row)
    strict = jj < ii

    d0 = decay_ref[...]
    d_hi = d0.astype(BF16)
    rest = d0 - d_hi.astype(F32)
    d_mid = rest.astype(BF16)
    d_lo = (rest - d_mid.astype(F32)).astype(BF16)
    upper_ones = (ii <= jj).astype(F32).astype(BF16)
    pieces = jnp.concatenate([d_hi.astype(F32), d_mid.astype(F32), d_lo.astype(F32), jnp.zeros((10, TOK), F32)], axis=0)
    sums = dot(pieces.astype(BF16), upper_ones)
    cum = sums[0:2] + sums[2:4] + sums[4:6]

    kf = dk_ref[...].astype(F32)
    qf = dq_ref[...].astype(F32)
    rk_col = lax.rsqrt(jnp.sum(kf * kf, axis=1, keepdims=True) + EPS)
    rq_col = lax.rsqrt(jnp.sum(qf * qf, axis=1, keepdims=True) + EPS)
    rk_row = jnp.broadcast_to(rk_col, (TOK, DHD)).T[0:1]
    packed = jnp.concatenate([cum, beta_ref[...], jnp.zeros((DHD - 4, TOK), F32)], axis=0).T
    kk = dot(dk_ref[...], dk_ref[...], NT) * rk_col * rk_row
    qk = dot(dq_ref[...], dk_ref[...], NT) * rq_col * rk_row
    tick()

    decays, lows = [], []
    for h in range(2):
        diff = packed[:, h : h + 1] - cum[h : h + 1]
        decay = jnp.where(lower, jnp.exp(jnp.where(lower, diff, 0.0)), 0.0)
        decays.append(decay)
        lows.append(jnp.where(strict, packed[:, 2 + h : 3 + h] * decay * kk, 0.0))
    tick()

    eye = (ii == jj).astype(F32)
    inverses = None
    size = 1
    while size < TOK:
        cross = (ii // (2 * size) == jj // (2 * size)) & (ii // size != jj // size)
        if size == 1:
            inverses = [eye - jnp.where(cross, low, 0.0) for low in lows]
        else:
            parts = [split(t) for t in inverses]
            inner = [dot3(split(jnp.where(cross, low, 0.0)), t) for low, t in zip(lows, parts)]
            inverses = [t - dot3(tp, split(m)) for t, tp, m in zip(inverses, parts, inner)]
            tick()
        size *= 2

    k_raw = dk_ref[...]
    k_t = kf.T.astype(BF16)
    sub = lax.broadcasted_iota(jnp.int32, (16, DHD), 0)
    for h in range(2):
        alive_row = (pid_row == pid_before).astype(F32)
        alive_col = (pid_col == pid_before).astype(F32)
        growth_row = jnp.exp(cum[h : h + 1]) * alive_row
        growth_col = jnp.exp(packed[:, h : h + 1]) * alive_col
        beta_row = beta_ref[h : h + 1, :]
        u = dot2(split(inverses[h] * beta_row), dv_ref[:, h * DHD : (h + 1) * DHD])
        w = dot2(split(inverses[h] * (beta_row * growth_row * rk_row)), k_raw)
        wu = jnp.concatenate([w, u], axis=1)
        last = cum[h : h + 1, TOK - 1 : TOK]
        tail = jnp.where(pid_col == pid_last, jnp.exp(last - packed[:, h : h + 1]), 0.0) * rk_col
        tw = split(wu * tail)
        maps = dot(k_t, tw[0]) + dot(k_t, tw[1])
        gamma = jnp.broadcast_to(growth_row[:, TOK - 1 : TOK], (1, DHD))
        g_hi = gamma.astype(BF16).astype(F32)
        own[h, 0:DHD] = maps[:, :DHD]
        own[h, DHD : 2 * DHD] = maps[:, DHD:]
        own[h, 2 * DHD :] = jnp.where(sub == 0, g_hi, jnp.where(sub == 1, gamma - g_hi, 0.0))
        csend[0, h] = own[h].astype(BF16)
        pw = dot3(split(qk * decays[h]), split(wu))
        eff[h, :, :DHD] = (growth_col * rq_col) * qf - pw[:, :DHD]
        eff[h, :, DHD:] = pw[:, DHD:]
        tick()

    def chain_send(step, slot, distance):
        return copy(csend.at[step], crecv.at[slot], c_s.at[slot], c_r.at[slot], grp, ctx + distance)

    def chain_start(step, slot, distance):
        @pl.when(ctx + distance < 32)
        def _():
            chain_send(step, slot, distance).start()

    def chain_wait(slot, distance):
        @pl.when(ctx >= distance)
        def _():
            arrived(crecv.at[slot], c_r.at[slot])

        @pl.when(ctx < distance)
        def _():
            crecv[slot] = jnp.zeros((2, MSG, DHD), BF16)

    def unpack(message):
        gamma = jnp.sum(message[2 * DHD :].astype(F32), axis=0, keepdims=True)
        return message[0:DHD], message[DHD : 2 * DHD], gamma

    def compose(later, earlier, maps=True):
        g2, o2, y2 = later
        g1, o1, y1 = earlier
        if not maps:
            return None, y2 * o1.astype(F32) - dot(g2, o1) + o2.astype(F32), None
        both = dot(g2, jnp.concatenate([g1, o1], axis=1))
        g = y2 * g1.astype(F32) + y1 * g2.astype(F32) - both[:, :DHD]
        o = y2 * o1.astype(F32) - both[:, DHD:] + o2.astype(F32)
        return g, o, y2 * y1

    def pack(step, h, g, o, gamma):
        g_hi = gamma.astype(BF16).astype(F32)
        csend[step, h, 0:DHD] = g.astype(BF16)
        csend[step, h, DHD : 2 * DHD] = o.astype(BF16)
        csend[step, h, 2 * DHD :] = jnp.where(sub == 0, g_hi, jnp.where(sub == 1, gamma - g_hi, 0.0)).astype(BF16)

    chain_start(0, 0, 1)
    chain_start(0, 1, 2)

    acc[...] = jnp.zeros_like(acc)
    for hh in range(4):
        stat[hh, 0:1] = jnp.full((1, TOK), START_MAX, F32)
        stat[hh, 1:2] = jnp.zeros((1, TOK), F32)
    quad_ready = [False]

    def attend(dy):
        tick_through(dy)
        if not quad_ready[0]:
            quad_ready[0] = True
            for i in range(3):
                arrived(qall.at[quad_member[i]], q_r.at[i])

        @pl.when(y >= dy)
        def _():
            key_pos = ((y - dy) * 4 + col_i // PIECE) * TOK + member * PIECE + col_i % PIECE
            keep = (key_pos <= first + row_i) & (prompt(key_pos) == pid_row)
            bias[...] = jnp.where(keep, 0.0, MASKED)
            keys = kv[dy, 0].reshape(TOK, HD)
            vals_t = kv[dy, 1].reshape(TOK, HD).T

            def one(hh, carry):
                s = dot(keys, qall[hh], NT) + bias[...]
                old = stat[hh, 0:1]
                new = jnp.maximum(old, jnp.max(s, axis=0, keepdims=True))
                scale = jnp.exp(old - new)
                p = jnp.exp(s - new)
                stat[hh, 0:1] = new
                stat[hh, 1:2] = stat[hh, 1:2] * scale + jnp.sum(p, axis=0, keepdims=True)
                acc[hh] = acc[hh] * scale + dot(vals_t, p.astype(BF16))
                return carry

            lax.fori_loop(0, 4, one, 0)

    attend(0)
    chain_wait(0, 1)
    chain_wait(1, 2)
    for h in range(2):
        pack(1, h, *compose(unpack(crecv[0, h]), unpack(crecv[1, h])))
    chain_start(1, 2, 2)
    attend(1)
    chain_wait(2, 2)
    for h in range(2):
        pack(2, h, *compose(unpack(csend[1, h]), unpack(crecv[2, h])))
    chain_start(2, 3, 4)
    attend(2)
    chain_wait(3, 4)
    for h in range(2):
        pack(3, h, *compose(unpack(csend[2, h]), unpack(crecv[3, h])))
    chain_start(3, 4, 8)
    attend(3)
    attend(4)

    for i in (1, 2, 0):
        accs[i] = acc[quad_member[i]].astype(BF16)
        stats[i] = stat[quad_member[i]]
        copy(stats.at[i], statr.at[i], t_s.at[i], t_r.at[i], quad_grp[i], ctx).start()
        copy(accs.at[i], accr.at[i], a_s.at[i], a_r.at[i], quad_grp[i], ctx).start()

    def project(p, heads, w_ref, w_copy):
        w_copy.wait()
        for b in range(8):
            part = dot(heads, w_ref[:, b * 256 : (b + 1) * 256]).astype(BF16)
            pbuf[p, 0, b] = part[:, :DHD]
            pbuf[p, 1, b] = part[:, DHD:]
            i = p * 8 + b
            copy(pbuf.at[p, 1 - c, b], r1.at[p, b], s1_s.at[i], s1_r.at[i], sib_grp, ctx).start()

    def pair_sum(p, b):
        arrived(r1.at[p, b], s1_r.at[p * 8 + b])
        return pbuf[p, c, b].astype(F32) + r1[p, b].astype(F32)

    def across_x(p):
        for d in (2, 1, 3):
            xd = (x + d) % 4
            for e in range(2):
                s2[p, d - 1, e] = pair_sum(p, xd * 2 + e).astype(BF16)
            i = p * 3 + d - 1
            copy(s2.at[p, d - 1], r2.at[p, d - 1], s2_s.at[i], s2_r.at[i], x_grp[d - 1], ctx).start()

    def across_z(p):
        far = pair_sum(p, x * 2 + 1 - zh)
        near = pair_sum(p, x * 2 + zh)
        for d in (1, 3, 2):
            arrived(r2.at[p, d - 1], s2_r.at[p * 3 + d - 1])
            far += r2[p, d - 1, 1 - zh].astype(F32)
            near += r2[p, d - 1, zh].astype(F32)
        s3[p] = far.astype(BF16)
        copy(s3.at[p], r3.at[p], s3_s.at[p], s3_r.at[p], z_grp, ctx).start()
        return near

    def finish(p, near, o_ref):
        arrived(r3.at[p], s3_r.at[p])
        o_ref[...] = (near + r3[p].astype(F32)).astype(BF16)

    maxes, sums_, parts = [], [], []
    for i in range(3):
        arrived(statr.at[i], t_r.at[i])
    top = stat[member, 0:1]
    for i in range(3):
        top = jnp.maximum(top, statr[i, 0:1])
    scale = jnp.exp(stat[member, 0:1] - top)
    total = stat[member, 1:2] * scale
    mixed = acc[member] * scale
    for i in (0, 1, 2):
        arrived(accr.at[i], a_r.at[i])
        scale = jnp.exp(statr[i, 0:1] - top)
        total += statr[i, 1:2] * scale
        mixed += accr[i].astype(F32) * scale
    core_out = (mixed / total).T
    attn_heads = (core_out * jax.nn.sigmoid(agate_ref[...].astype(F32))).astype(BF16)
    project(0, attn_heads, wa_ref, wa_copy)

    chain_wait(4, 8)
    heads = []
    across_x(0)
    for h in range(2):
        _, state, _ = compose(unpack(csend[3, h]), unpack(crecv[4, h]), maps=False)
        core = dot3(split(eff[h, :, :DHD]), split(state)) + eff[h, :, DHD:]
        squares = jnp.mean(core * core, axis=1, keepdims=True)
        gate = dgate_ref[:, h * DHD : (h + 1) * DHD].astype(F32)
        normed = core * lax.rsqrt(squares + EPS) * gain_ref[...]
        heads.append((normed * gate * jax.nn.sigmoid(gate)).astype(BF16))
    project(1, jnp.concatenate(heads, axis=1), wd_ref, wd_copy)
    near_a = across_z(0)
    across_x(1)
    finish(0, near_a, oa_ref)
    near_d = across_z(1)
    finish(1, near_d, od_ref)

    for i in range(3):
        copy(kv.at[0, :, z], kv.at[0, :, z], z_s.at[i], kv_r.at[z], grp, row_ctx[i]).wait_send()
        copy(qall.at[member], qall.at[member], q_s.at[i], q_r.at[i], quad_grp[i], ctx).wait_send()
        copy(stats.at[i], statr.at[i], t_s.at[i], t_r.at[i], quad_grp[i], ctx).wait_send()
        copy(accs.at[i], accr.at[i], a_s.at[i], a_r.at[i], quad_grp[i], ctx).wait_send()
    for dy in range(4):

        @pl.when((y >= dy) & (y < 7))
        def _():
            for zs in range(4):
                forward(dy, zs).wait_send()

    for step, slot, distance in ((0, 0, 1), (0, 1, 2), (1, 2, 2), (2, 3, 4), (3, 4, 8)):

        @pl.when(ctx + distance < 32)
        def _():
            chain_send(step, slot, distance).wait_send()

    for p in range(2):
        for b in range(8):
            i = p * 8 + b
            copy(pbuf.at[p, 1 - c, b], r1.at[p, b], s1_s.at[i], s1_r.at[i], sib_grp, ctx).wait_send()
        for d in range(3):
            i = p * 3 + d
            copy(s2.at[p, d], r2.at[p, d], s2_s.at[i], s2_r.at[i], x_grp[d], ctx).wait_send()
        copy(s3.at[p], r3.at[p], s3_s.at[p], s3_r.at[p], z_grp, ctx).wait_send()


def local(
    queries,
    keys,
    values,
    attn_gate,
    delta_query,
    delta_key,
    delta_value,
    delta_gate,
    decay_log,
    beta,
    norm_gain,
    attn_out_weight,
    delta_out_weight,
    doc_lengths,
):
    ends = (jnp.cumsum(doc_lengths) * BLOCK).astype(jnp.int32)
    vmem = pl.BlockSpec(memory_space=pltpu.VMEM)
    anywhere = pl.BlockSpec(memory_space=pl.ANY)
    dma = lambda n: pltpu.SemaphoreType.DMA((n,))
    out = jax.ShapeDtypeStruct((TOK, DHD), BF16)
    return pl.pallas_call(
        kernel,
        out_shape=(out, out),
        in_specs=[pl.BlockSpec(memory_space=pltpu.SMEM)] + [vmem] * 11 + [anywhere] * 2,
        out_specs=(vmem, vmem),
        scratch_shapes=[
            pltpu.VMEM((256, 2048), BF16),
            pltpu.VMEM((256, 2048), BF16),
            pltpu.VMEM((4, TOK, HD), BF16),
            pltpu.VMEM((5, 2, 4, PIECE, HD), BF16),
            pltpu.VMEM((TOK, TOK), F32),
            pltpu.VMEM((4, HD, TOK), F32),
            pltpu.VMEM((4, 8, TOK), F32),
            pltpu.VMEM((3, HD, TOK), BF16),
            pltpu.VMEM((3, HD, TOK), BF16),
            pltpu.VMEM((3, 8, TOK), F32),
            pltpu.VMEM((3, 8, TOK), F32),
            pltpu.VMEM((2, MSG, DHD), F32),
            pltpu.VMEM((4, 2, MSG, DHD), BF16),
            pltpu.VMEM((5, 2, MSG, DHD), BF16),
            pltpu.VMEM((2, TOK, 2 * DHD), F32),
            pltpu.VMEM((2, 2, 8, TOK, DHD), BF16),
            pltpu.VMEM((2, 8, TOK, DHD), BF16),
            pltpu.VMEM((2, 3, 2, TOK, DHD), BF16),
            pltpu.VMEM((2, 3, 2, TOK, DHD), BF16),
            pltpu.VMEM((2, TOK, DHD), BF16),
            pltpu.VMEM((2, TOK, DHD), BF16),
            dma(2),
            dma(3),
            dma(3),
            dma(3),
            dma(16),
            dma(20),
            dma(5),
            dma(5),
            dma(3),
            dma(3),
            dma(3),
            dma(3),
            dma(16),
            dma(16),
            dma(6),
            dma(6),
            dma(2),
            dma(2),
        ],
        compiler_params=pltpu.CompilerParams(
            collective_id=0, has_side_effects=True, vmem_limit_bytes=48 * 1024 * 1024
        ),
        cost_estimate=pl.CostEstimate(flops=4 * 10**9, bytes_accessed=6 * 10**6, transcendentals=2 * 10**6),
    )(
        ends,
        queries,
        keys,
        values,
        attn_gate,
        delta_query,
        delta_key,
        delta_value,
        delta_gate,
        decay_log,
        beta,
        norm_gain.reshape(1, DHD),
        attn_out_weight,
        delta_out_weight,
    )


def solution(mesh):
    placed = (
        P("ctx", "grp"),
        P("ctx", None),
        P("ctx", None),
        P("ctx", "grp"),
        P("ctx", "grp"),
        P("ctx", "grp"),
        P("ctx", "grp"),
        P("ctx", "grp"),
        P("grp", "ctx"),
        P("grp", "ctx"),
        P(),
        P("grp", None),
        P("grp", None),
        P(),
    )
    return jax.shard_map(
        local,
        mesh=mesh,
        in_specs=placed,
        out_specs=(P("ctx", "grp"), P("ctx", "grp")),
        check_vma=False,
    )
```

```python
import functools

import jax
import jax.numpy as jnp
from jax import lax
from jax.experimental import pallas as pl
from jax.experimental.pallas import tpu as pltpu
from jax.sharding import PartitionSpec as P

MESH = pl.DeviceIdType.MESH
F32 = jnp.float32
BF16 = jnp.bfloat16

HEADS = 16
HD = 256
KVH = 2
DHD = 128
BLOCK = 64
TOK = 256
PIECE = 64
MSG = 2 * DHD + 16

EPS = 1e-06
MASKED = -2e30
START_MAX = -1e30

NT = (((1,), (1,)), ((), ()))
NN = (((1,), (0,)), ((), ()))


def dot(a, b, dims=NN):
    return lax.dot_general(a, b, dims, preferred_element_type=F32)


def split(x):
    high = x.astype(BF16)
    return high, (x - high.astype(F32)).astype(BF16)


def dot3(a, b):
    ah, al = a
    bh, bl = b
    return dot(ah, bh) + (dot(ah, bl) + dot(al, bh))


def dot2(a, b):
    return dot(a[0], b) + dot(a[1], b)


def kernel(
    lengths_ref,
    q_hbm,
    k_hbm,
    v_hbm,
    agate_hbm,
    dq_hbm,
    dk_hbm,
    dv_hbm,
    dgate_hbm,
    decay_hbm,
    beta_hbm,
    gain_hbm,
    wa_hbm,
    wd_hbm,
    oa_ref,
    od_ref,
    q_ref,
    agate_ref,
    dq_ref,
    dk_ref,
    dv_ref,
    dgate_ref,
    decay_ref,
    beta_ref,
    gain_ref,
    wa_ref,
    wd_ref,
    qall,
    kv,
    bias,
    acc,
    stat,
    accs,
    accr,
    stats,
    statr,
    own,
    csend,
    crecv,
    eff,
    pbuf,
    r1,
    s2,
    r2,
    s3,
    r3,
    w_sem,
    q_s,
    q_r,
    z_s,
    y_s,
    kv_r,
    c_s,
    c_r,
    a_s,
    a_r,
    t_s,
    t_r,
    s1_s,
    s1_r,
    s2_s,
    s2_r,
    s3_s,
    s3_r,
):
    grp = lax.axis_index("grp")
    ctx = lax.axis_index("ctx")
    x, zh, c = grp // 4, (grp // 2) % 2, grp % 2
    y, z = ctx // 4, ctx % 4
    xb = x % 2
    kvh = x // 2
    member = xb * 2 + c

    def grp_of(x_, zh_, c_):
        return x_ * 4 + zh_ * 2 + c_

    xn = x + 1 - 2 * xb
    quad = [(x, 1 - c), (xn, c), (xn, 1 - c)]
    quad_grp = [grp_of(a, zh, b) for a, b in quad]
    quad_member = [(a % 2) * 2 + b for a, b in quad]
    x_grp = [grp_of((x + d) % 4, zh, c) for d in (1, 2, 3)]
    z_grp = grp_of(x, 1 - zh, c)
    sib_grp = quad_grp[0]
    row_ctx = [y * 4 + (z + d) % 4 for d in (1, 2, 3)]

    def copy(src, dst, send, recv, g, r):
        return pltpu.make_async_remote_copy(
            src_ref=src,
            dst_ref=dst,
            send_sem=send,
            recv_sem=recv,
            device_id={"grp": g, "ctx": r},
            device_id_type=MESH,
        )

    def arrived(dst, sem):
        pltpu.make_async_copy(dst, dst, sem).wait()

    sends = []

    barrier = pltpu.get_barrier_semaphore()
    peers = [(g, ctx) for g in quad_grp + x_grp + [z_grp]]
    peers += [(grp, r) for r in row_ctx]
    peers += [(grp, (ctx + d) % 32) for d in (1, 31, 2, 30, 4, 28, 8, 24)]
    for g, r in peers:
        pl.semaphore_signal(barrier, inc=1, device_id={"grp": g, "ctx": r}, device_id_type=MESH)

    rows = pl.ds(pl.multiple_of(member * PIECE, PIECE), PIECE)
    cols = pl.ds(pl.multiple_of(kvh * HD, HD), HD)
    loads = [
        pltpu.make_async_copy(src, dst, w_sem.at[i])
        for i, (src, dst) in enumerate(
            [
                (k_hbm.at[rows, cols], kv.at[0, 0, z]),
                (v_hbm.at[rows, cols], kv.at[0, 1, z]),
                (q_hbm, q_ref),
                (dk_hbm, dk_ref),
                (dq_hbm, dq_ref),
                (decay_hbm, decay_ref),
                (beta_hbm, beta_ref),
                (dv_hbm, dv_ref),
                (gain_hbm, gain_ref),
                (dgate_hbm, dgate_ref),
                (agate_hbm, agate_ref),
                (wd_hbm, wd_ref),
                (wa_hbm, wa_ref),
            ]
        )
    ]
    for load in loads:
        load.start()
    for load in loads[:3]:
        load.wait()
    qall[member] = q_ref[...] * jnp.asarray(HD ** (-0.5), BF16)
    pl.semaphore_wait(barrier, len(peers))

    def forward(dy, zs):
        return copy(
            kv.at[dy, :, zs], kv.at[dy + 1, :, zs], y_s.at[dy * 4 + zs], kv_r.at[dy * 4 + 4 + zs], grp, ctx + 4
        )

    @pl.when(y < 7)
    def _():
        forward(0, z).start()

    for i in range(3):
        copy(kv.at[0, :, z], kv.at[0, :, z], z_s.at[i], kv_r.at[z], grp, row_ctx[i]).start()
    for i in (1, 2, 0):
        copy(qall.at[member], qall.at[member], q_s.at[i], q_r.at[i], quad_grp[i], ctx).start()

    ticks = [(1, 0), (0, 1), (0, 2), (0, 3), (2, 0), (1, 1), (1, 2), (1, 3), (3, 0), (2, 1)]
    ticks += [(2, 2), (2, 3), (4, 0), (3, 1), (3, 2), (3, 3), (4, 1), (4, 2), (4, 3)]

    def tick(count=1):
        for _ in range(count):
            if not ticks:
                return
            dy, i = ticks.pop(0)
            zs = (z + i) % 4

            @pl.when(y >= dy)
            def _():
                arrived(kv.at[dy, :, zs], kv_r.at[dy * 4 + zs])

                if dy < 4:

                    @pl.when(y < 7)
                    def _():
                        forward(dy, zs).start()

    def tick_through(dy):
        while any(t[0] <= dy for t in ticks):
            tick()

    first = ctx * TOK
    ends = [lengths_ref[0] * BLOCK]
    for i in range(1, 4):
        ends.append(ends[-1] + lengths_ref[i] * BLOCK)
    for load in loads[3:9]:
        load.wait()

    def prompt(pos):
        total = (pos >= ends[0]).astype(F32)
        for e in ends[1:]:
            total += (pos >= e).astype(F32)
        return total

    row_i = lax.broadcasted_iota(jnp.int32, (1, TOK), 1)
    col_i = lax.broadcasted_iota(jnp.int32, (TOK, 1), 0)
    pid_row = prompt(first + row_i)
    pid_col = prompt(first + col_i)
    pid_before = prompt(jnp.full((1, 1), first - 1, jnp.int32))
    pid_last = prompt(jnp.full((1, 1), first + TOK - 1, jnp.int32))

    ii = lax.broadcasted_iota(jnp.int32, (TOK, TOK), 0)
    jj = lax.broadcasted_iota(jnp.int32, (TOK, TOK), 1)
    lower = (jj <= ii) & (pid_col == pid_row)
    strict = jj < ii

    d0 = decay_ref[...]
    d_hi = d0.astype(BF16)
    rest = d0 - d_hi.astype(F32)
    d_mid = rest.astype(BF16)
    d_lo = (rest - d_mid.astype(F32)).astype(BF16)
    upper_ones = (ii <= jj).astype(F32).astype(BF16)
    pieces = jnp.concatenate([d_hi.astype(F32), d_mid.astype(F32), d_lo.astype(F32), jnp.zeros((10, TOK), F32)], axis=0)
    sums = dot(pieces.astype(BF16), upper_ones)
    cum = sums[0:2] + sums[2:4] + sums[4:6]

    kf = dk_ref[...].astype(F32)
    qf = dq_ref[...].astype(F32)
    rk_col = lax.rsqrt(jnp.sum(kf * kf, axis=1, keepdims=True) + EPS)
    rq_col = lax.rsqrt(jnp.sum(qf * qf, axis=1, keepdims=True) + EPS)
    rk_row = jnp.broadcast_to(rk_col, (TOK, DHD)).T[0:1]
    packed = jnp.concatenate([cum, beta_ref[...], jnp.zeros((DHD - 4, TOK), F32)], axis=0).T
    kk = dot(dk_ref[...], dk_ref[...], NT) * rk_col * rk_row
    qk = dot(dq_ref[...], dk_ref[...], NT) * rq_col * rk_row

    decays, lows = [], []
    for h in range(2):
        diff = packed[:, h : h + 1] - cum[h : h + 1]
        decay = jnp.where(lower, jnp.exp(jnp.where(lower, diff, 0.0)), 0.0)
        decays.append(decay)
        lows.append(jnp.where(strict, packed[:, 2 + h : 3 + h] * decay * kk, 0.0))

    eye = (ii == jj).astype(F32)
    inverses = None
    size = 1
    while size < TOK:
        cross = (ii // (2 * size) == jj // (2 * size)) & (ii // size != jj // size)
        if size == 1:
            inverses = [eye - jnp.where(cross, low, 0.0) for low in lows]
        else:
            parts = [split(t) for t in inverses]
            inner = [dot3(split(jnp.where(cross, low, 0.0)), t) for low, t in zip(lows, parts)]
            inverses = [t - dot3(tp, split(m)) for t, tp, m in zip(inverses, parts, inner)]
            if size >= 32:
                tick()
        size *= 2

    k_raw = dk_ref[...]
    k_t = kf.T.astype(BF16)
    sub = lax.broadcasted_iota(jnp.int32, (16, DHD), 0)
    for h in range(2):
        alive_row = (pid_row == pid_before).astype(F32)
        alive_col = (pid_col == pid_before).astype(F32)
        growth_row = jnp.exp(cum[h : h + 1]) * alive_row
        growth_col = jnp.exp(packed[:, h : h + 1]) * alive_col
        beta_row = beta_ref[h : h + 1, :]
        u = dot2(split(inverses[h] * beta_row), dv_ref[:, h * DHD : (h + 1) * DHD])
        w = dot2(split(inverses[h] * (beta_row * growth_row * rk_row)), k_raw)
        wu = jnp.concatenate([w, u], axis=1)
        last = cum[h : h + 1, TOK - 1 : TOK]
        tail = jnp.where(pid_col == pid_last, jnp.exp(last - packed[:, h : h + 1]), 0.0) * rk_col
        tw = split(wu * tail)
        maps = dot(k_t, tw[0]) + dot(k_t, tw[1])
        gamma = jnp.broadcast_to(growth_row[:, TOK - 1 : TOK], (1, DHD))
        g_hi = gamma.astype(BF16).astype(F32)
        own[h, 0:DHD] = maps[:, :DHD]
        own[h, DHD : 2 * DHD] = maps[:, DHD:]
        own[h, 2 * DHD :] = jnp.where(sub == 0, g_hi, jnp.where(sub == 1, gamma - g_hi, 0.0))
        csend[0, h] = own[h].astype(BF16)
        pw = dot3(split(qk * decays[h]), split(wu))
        eff[h, :, :DHD] = (growth_col * rq_col) * qf - pw[:, :DHD]
        eff[h, :, DHD:] = pw[:, DHD:]

    def chain_send(step, slot, distance):
        part = pl.ds(0, MSG) if distance < 8 else pl.ds(DHD, DHD)
        src, dst = csend.at[step, :, part], crecv.at[slot, :, part]
        return copy(src, dst, c_s.at[slot], c_r.at[slot], grp, ctx + distance)

    def chain_start(step, slot, distance):
        @pl.when(ctx + distance < 32)
        def _():
            chain_send(step, slot, distance).start()

    def chain_wait(slot, distance):
        @pl.when(ctx >= distance)
        def _():
            part = pl.ds(0, MSG) if distance < 8 else pl.ds(DHD, DHD)
            arrived(crecv.at[slot, :, part], c_r.at[slot])

        @pl.when(ctx < distance)
        def _():
            crecv[slot] = jnp.zeros((2, MSG, DHD), BF16)

    def unpack(message):
        gamma = jnp.sum(message[2 * DHD :].astype(F32), axis=0, keepdims=True)
        return message[0:DHD], message[DHD : 2 * DHD], gamma

    def apply_map(later, o1):
        g2, o2, y2 = later
        return y2 * o1.astype(F32) - dot(g2, o1) + o2.astype(F32)

    def compose(later, earlier):
        g2, o2, y2 = later
        g1, o1, y1 = earlier
        both = dot(g2, jnp.concatenate([g1, o1], axis=1))
        g = y2 * g1.astype(F32) + y1 * g2.astype(F32) - both[:, :DHD]
        o = y2 * o1.astype(F32) - both[:, DHD:] + o2.astype(F32)
        return g, o, y2 * y1

    def pack(step, h, g, o, gamma):
        g_hi = gamma.astype(BF16).astype(F32)
        csend[step, h, 0:DHD] = g.astype(BF16)
        csend[step, h, DHD : 2 * DHD] = o.astype(BF16)
        csend[step, h, 2 * DHD :] = jnp.where(sub == 0, g_hi, jnp.where(sub == 1, gamma - g_hi, 0.0)).astype(BF16)

    chain_start(0, 0, 1)
    chain_start(0, 1, 2)

    acc[...] = jnp.zeros_like(acc)
    for hh in range(4):
        stat[hh, 0:1] = jnp.full((1, TOK), START_MAX, F32)
        stat[hh, 1:2] = jnp.zeros((1, TOK), F32)
    quad_ready = [False]

    heads_order = [quad_member[1], quad_member[2], quad_member[0], member]

    def attend(dy, then=None):
        tick_through(dy)
        if not quad_ready[0]:
            quad_ready[0] = True
            for i in range(3):
                arrived(qall.at[quad_member[i]], q_r.at[i])

        def masks():
            key_pos = ((y - dy) * 4 + col_i // PIECE) * TOK + member * PIECE + col_i % PIECE
            keep = (key_pos <= first + row_i) & (prompt(key_pos) == pid_row)
            bias[...] = jnp.where(keep, 0.0, MASKED)

        def one(hh):
            keys = kv[dy, 0].reshape(TOK, HD)
            s = dot(keys, qall[hh], NT) + bias[...]
            old = stat[hh, 0:1]
            new = jnp.maximum(old, jnp.max(s, axis=0, keepdims=True))
            scale = jnp.exp(old - new)
            p = jnp.exp(s - new)
            stat[hh, 0:1] = new
            stat[hh, 1:2] = stat[hh, 1:2] * scale + jnp.sum(p, axis=0, keepdims=True)
            vals_t = kv[dy, 1].reshape(TOK, HD).T
            acc[hh] = acc[hh] * scale + dot(vals_t, p.astype(BF16))

        pl.when(y >= dy)(masks)
        for n, hh in enumerate(heads_order):
            pl.when(y >= dy)(functools.partial(one, hh))
            if then is not None:
                then(n)
            else:
                tick()

    attend(0)
    chain_wait(0, 1)
    chain_wait(1, 2)
    for h in range(2):
        pack(1, h, *compose(unpack(crecv[0, h]), unpack(crecv[1, h])))
    chain_start(1, 2, 2)
    attend(1)
    chain_wait(2, 2)
    for h in range(2):
        pack(2, h, *compose(unpack(csend[1, h]), unpack(crecv[2, h])))
    chain_start(2, 3, 4)
    attend(2)
    chain_wait(3, 4)
    for h in range(2):
        pack(3, h, *compose(unpack(csend[2, h]), unpack(crecv[3, h])))
    chain_start(3, 4, 8)
    attend(3)

    def project(p, heads, w_ref):
        for b in range(8):
            part = dot(heads, w_ref[:, b * 256 : (b + 1) * 256]).astype(BF16)
            pbuf[p, 0, b] = part[:, :DHD]
            pbuf[p, 1, b] = part[:, DHD:]
            i = p * 8 + b
            copy(pbuf.at[p, 1 - c, b], r1.at[p, b], s1_s.at[i], s1_r.at[i], sib_grp, ctx).start()

    def pair_sum(p, b):
        arrived(r1.at[p, b], s1_r.at[p * 8 + b])
        return pbuf[p, c, b].astype(F32) + r1[p, b].astype(F32)

    def across_x(p):
        for d in (2, 1, 3):
            xd = (x + d) % 4
            for e in range(2):
                s2[p, d - 1, e] = pair_sum(p, xd * 2 + e).astype(BF16)
            i = p * 3 + d - 1
            copy(s2.at[p, d - 1], r2.at[p, d - 1], s2_s.at[i], s2_r.at[i], x_grp[d - 1], ctx).start()

    def across_z(p):
        far = pair_sum(p, x * 2 + 1 - zh)
        near = pair_sum(p, x * 2 + zh)
        for d in (1, 3, 2):
            arrived(r2.at[p, d - 1], s2_r.at[p * 3 + d - 1])
            far += r2[p, d - 1, 1 - zh].astype(F32)
            near += r2[p, d - 1, zh].astype(F32)
        s3[p] = far.astype(BF16)
        copy(s3.at[p], r3.at[p], s3_s.at[p], s3_r.at[p], z_grp, ctx).start()
        return near

    def finish(p, near, o_ref):
        arrived(r3.at[p], s3_r.at[p])
        o_ref[...] = (near + r3[p].astype(F32)).astype(BF16)

    for load in (loads[9], loads[11]):
        load.wait()
    chain_wait(4, 8)
    heads = []
    for h in range(2):
        state = apply_map(unpack(csend[3, h]), crecv[4, h, DHD : 2 * DHD])
        core = dot3(split(eff[h, :, :DHD]), split(state)) + eff[h, :, DHD:]
        squares = jnp.mean(core * core, axis=1, keepdims=True)
        gate = dgate_ref[:, h * DHD : (h + 1) * DHD].astype(F32)
        normed = core * lax.rsqrt(squares + EPS) * gain_ref[...]
        heads.append((normed * gate * jax.nn.sigmoid(gate)).astype(BF16))
    project(1, jnp.concatenate(heads, axis=1), wd_ref)
    tick(4)

    def send_partial(n):
        if n == 3:
            return
        i = (1, 2, 0)[n]
        accs[i] = acc[quad_member[i]].astype(BF16)
        stats[i] = stat[quad_member[i]]
        copy(stats.at[i], statr.at[i], t_s.at[i], t_r.at[i], quad_grp[i], ctx).start()
        copy(accs.at[i], accr.at[i], a_s.at[i], a_r.at[i], quad_grp[i], ctx).start()

    attend(4, send_partial)
    across_x(1)
    for load in (loads[10], loads[12]):
        load.wait()
    for i in range(3):
        arrived(statr.at[i], t_r.at[i])
    top = stat[member, 0:1]
    for i in range(3):
        top = jnp.maximum(top, statr[i, 0:1])
    scale = jnp.exp(stat[member, 0:1] - top)
    total = stat[member, 1:2] * scale
    mixed = acc[member] * scale
    for i in (0, 1, 2):
        arrived(accr.at[i], a_r.at[i])
        scale = jnp.exp(statr[i, 0:1] - top)
        total += statr[i, 1:2] * scale
        mixed += accr[i].astype(F32) * scale
    core_out = (mixed / total).T
    attn_heads = (core_out * jax.nn.sigmoid(agate_ref[...].astype(F32))).astype(BF16)
    project(0, attn_heads, wa_ref)
    near_d = across_z(1)
    across_x(0)
    finish(1, near_d, od_ref)
    near_a = across_z(0)
    finish(0, near_a, oa_ref)

    for i in range(3):
        copy(kv.at[0, :, z], kv.at[0, :, z], z_s.at[i], kv_r.at[z], grp, row_ctx[i]).wait_send()
        copy(qall.at[member], qall.at[member], q_s.at[i], q_r.at[i], quad_grp[i], ctx).wait_send()
        copy(stats.at[i], statr.at[i], t_s.at[i], t_r.at[i], quad_grp[i], ctx).wait_send()
        copy(accs.at[i], accr.at[i], a_s.at[i], a_r.at[i], quad_grp[i], ctx).wait_send()
    for dy in range(4):

        @pl.when((y >= dy) & (y < 7))
        def _():
            for zs in range(4):
                forward(dy, zs).wait_send()

    for step, slot, distance in ((0, 0, 1), (0, 1, 2), (1, 2, 2), (2, 3, 4), (3, 4, 8)):

        @pl.when(ctx + distance < 32)
        def _():
            chain_send(step, slot, distance).wait_send()

    for p in range(2):
        for b in range(8):
            i = p * 8 + b
            copy(pbuf.at[p, 1 - c, b], r1.at[p, b], s1_s.at[i], s1_r.at[i], sib_grp, ctx).wait_send()
        for d in range(3):
            i = p * 3 + d
            copy(s2.at[p, d], r2.at[p, d], s2_s.at[i], s2_r.at[i], x_grp[d], ctx).wait_send()
        copy(s3.at[p], r3.at[p], s3_s.at[p], s3_r.at[p], z_grp, ctx).wait_send()


def local(
    queries,
    keys,
    values,
    attn_gate,
    delta_query,
    delta_key,
    delta_value,
    delta_gate,
    decay_log,
    beta,
    norm_gain,
    attn_out_weight,
    delta_out_weight,
    doc_lengths,
):
    vmem = pl.BlockSpec(memory_space=pltpu.VMEM)
    anywhere = pl.BlockSpec(memory_space=pltpu.HBM)
    dma = lambda n: pltpu.SemaphoreType.DMA((n,))
    out = jax.ShapeDtypeStruct((TOK, DHD), BF16)
    return pl.pallas_call(
        kernel,
        out_shape=(out, out),
        in_specs=[pl.BlockSpec(memory_space=pltpu.SMEM)] + [anywhere] * 13,
        out_specs=(vmem, vmem),
        scratch_shapes=[
            pltpu.VMEM((TOK, HD), BF16),
            pltpu.VMEM((TOK, HD), BF16),
            pltpu.VMEM((TOK, DHD), BF16),
            pltpu.VMEM((TOK, DHD), BF16),
            pltpu.VMEM((TOK, 2 * DHD), BF16),
            pltpu.VMEM((TOK, 2 * DHD), BF16),
            pltpu.VMEM((2, TOK), F32),
            pltpu.VMEM((2, TOK), F32),
            pltpu.VMEM((1, DHD), F32),
            pltpu.VMEM((256, 2048), BF16),
            pltpu.VMEM((256, 2048), BF16),
            pltpu.VMEM((4, TOK, HD), BF16),
            pltpu.VMEM((5, 2, 4, PIECE, HD), BF16),
            pltpu.VMEM((TOK, TOK), F32),
            pltpu.VMEM((4, HD, TOK), F32),
            pltpu.VMEM((4, 8, TOK), F32),
            pltpu.VMEM((3, HD, TOK), BF16),
            pltpu.VMEM((3, HD, TOK), BF16),
            pltpu.VMEM((3, 8, TOK), F32),
            pltpu.VMEM((3, 8, TOK), F32),
            pltpu.VMEM((2, MSG, DHD), F32),
            pltpu.VMEM((4, 2, MSG, DHD), BF16),
            pltpu.VMEM((5, 2, MSG, DHD), BF16),
            pltpu.VMEM((2, TOK, 2 * DHD), F32),
            pltpu.VMEM((2, 2, 8, TOK, DHD), BF16),
            pltpu.VMEM((2, 8, TOK, DHD), BF16),
            pltpu.VMEM((2, 3, 2, TOK, DHD), BF16),
            pltpu.VMEM((2, 3, 2, TOK, DHD), BF16),
            pltpu.VMEM((2, TOK, DHD), BF16),
            pltpu.VMEM((2, TOK, DHD), BF16),
            dma(13),
            dma(3),
            dma(3),
            dma(3),
            dma(16),
            dma(20),
            dma(5),
            dma(5),
            dma(3),
            dma(3),
            dma(3),
            dma(3),
            dma(16),
            dma(16),
            dma(6),
            dma(6),
            dma(2),
            dma(2),
        ],
        compiler_params=pltpu.CompilerParams(
            collective_id=0, has_side_effects=True, vmem_limit_bytes=64 * 1024 * 1024
        ),
        cost_estimate=pl.CostEstimate(flops=4 * 10**9, bytes_accessed=6 * 10**6, transcendentals=2 * 10**6),
    )(
        doc_lengths,
        queries,
        keys,
        values,
        attn_gate,
        delta_query,
        delta_key,
        delta_value,
        delta_gate,
        decay_log,
        beta,
        norm_gain.reshape(1, DHD),
        attn_out_weight,
        delta_out_weight,
    )


def solution(mesh):
    placed = (
        P("ctx", "grp"),
        P("ctx", None),
        P("ctx", None),
        P("ctx", "grp"),
        P("ctx", "grp"),
        P("ctx", "grp"),
        P("ctx", "grp"),
        P("ctx", "grp"),
        P("grp", "ctx"),
        P("grp", "ctx"),
        P(),
        P("grp", None),
        P("grp", None),
        P(),
    )
    return jax.shard_map(
        local,
        mesh=mesh,
        in_specs=placed,
        out_specs=(P("ctx", "grp"), P("ctx", "grp")),
        check_vma=False,
    )
```

```python
import functools

import jax
import jax.numpy as jnp
from jax import lax
from jax.experimental import pallas as pl
from jax.experimental.pallas import tpu as pltpu
from jax.sharding import PartitionSpec as P

MESH = pl.DeviceIdType.MESH
F32 = jnp.float32
BF16 = jnp.bfloat16

HEADS = 16
HD = 256
KVH = 2
DHD = 128
BLOCK = 64
TOK = 256
PIECE = 64
QUARTER = DHD // 4
MSG = 2 * DHD + 16

EPS = 1e-06
MASKED = -2e30
START_MAX = -1e30

NT = (((1,), (1,)), ((), ()))
NN = (((1,), (0,)), ((), ()))


def dot(a, b, dims=NN):
    return lax.dot_general(a, b, dims, preferred_element_type=F32)


def split(x):
    high = x.astype(BF16)
    return high, (x - high.astype(F32)).astype(BF16)


def dot3(a, b):
    ah, al = a
    bh, bl = b
    return dot(ah, bh) + (dot(ah, bl) + dot(al, bh))


def dot2(a, b):
    return dot(a[0], b) + dot(a[1], b)


def kernel(
    lengths_ref,
    q_hbm,
    k_hbm,
    v_hbm,
    agate_hbm,
    dq_hbm,
    dk_hbm,
    dv_hbm,
    dgate_hbm,
    decay_hbm,
    beta_hbm,
    gain_hbm,
    wa_hbm,
    wd_hbm,
    oa_ref,
    od_ref,
    q_ref,
    agate_ref,
    dq_ref,
    dk_ref,
    dv_ref,
    dgate_ref,
    decay_ref,
    beta_ref,
    gain_ref,
    wa_ref,
    wd_ref,
    qall,
    kv,
    acc,
    stat,
    accs,
    accr,
    stats,
    statr,
    csend,
    crecv,
    tsend,
    trecv,
    tall,
    state,
    eff,
    pbuf,
    r1,
    s2,
    r2,
    s4,
    r4,
    s3,
    r3,
    w_sem,
    q_s,
    q_r,
    z_s,
    y_s,
    kv_r,
    c_s,
    c_r,
    h_s,
    h_r,
    g_s,
    g_r,
    a_s,
    a_r,
    t_s,
    t_r,
    s1_s,
    s1_r,
    s2_s,
    s2_r,
    s3_s,
    s3_r,
):
    grp = lax.axis_index("grp")
    ctx = lax.axis_index("ctx")
    x, zh, c = grp // 4, (grp // 2) % 2, grp % 2
    y, z = ctx // 4, ctx % 4
    xb = x % 2
    kvh = x // 2
    member = xb * 2 + c

    def grp_of(x_, zh_, c_):
        return x_ * 4 + zh_ * 2 + c_

    xn = x + 1 - 2 * xb
    quad = [(x, 1 - c), (xn, c), (xn, 1 - c)]
    quad_grp = [grp_of(a, zh, b) for a, b in quad]
    quad_member = [(a % 2) * 2 + b for a, b in quad]
    z_grp = grp_of(x, 1 - zh, c)
    sib_grp, xn_grp = quad_grp[0], quad_grp[1]
    xm = (x + 3 + 2 * xb) % 4
    xo = (x + 2) % 4
    xm_grp = grp_of(xm, zh, c)
    row_ctx = [y * 4 + (z + d) % 4 for d in (1, 2, 3)]

    def copy(src, dst, send, recv, g, r):
        return pltpu.make_async_remote_copy(
            src_ref=src,
            dst_ref=dst,
            send_sem=send,
            recv_sem=recv,
            device_id={"grp": g, "ctx": r},
            device_id_type=MESH,
        )

    def arrived(dst, sem):
        pltpu.make_async_copy(dst, dst, sem).wait()

    sends = []

    barrier = pltpu.get_barrier_semaphore()
    peers = [(g, ctx) for g in quad_grp + [xm_grp, z_grp]]
    peers += [(grp, r) for r in row_ctx]
    peers += [(grp, (ctx + d) % 32) for d in (4, 28)]
    for g, r in peers:
        pl.semaphore_signal(barrier, inc=1, device_id={"grp": g, "ctx": r}, device_id_type=MESH)

    rows = pl.ds(pl.multiple_of(member * PIECE, PIECE), PIECE)
    cols = pl.ds(pl.multiple_of(kvh * HD, HD), HD)
    loads = [
        pltpu.make_async_copy(src, dst, w_sem.at[i])
        for i, (src, dst) in enumerate(
            [
                (k_hbm.at[rows, cols], kv.at[0, 0, z]),
                (v_hbm.at[rows, cols], kv.at[0, 1, z]),
                (q_hbm, q_ref),
                (dk_hbm, dk_ref),
                (dq_hbm, dq_ref),
                (decay_hbm, decay_ref),
                (beta_hbm, beta_ref),
                (dv_hbm, dv_ref),
                (gain_hbm, gain_ref),
                (dgate_hbm, dgate_ref),
                (agate_hbm, agate_ref),
                (wd_hbm, wd_ref),
                (wa_hbm, wa_ref),
            ]
        )
    ]
    for load in loads:
        load.start()
    for load in loads[:3]:
        load.wait()
    qall[member] = q_ref[...] * jnp.asarray(HD ** (-0.5), BF16)
    pl.semaphore_wait(barrier, len(peers))

    def forward(dy, zs):
        return copy(
            kv.at[dy, :, zs], kv.at[dy + 1, :, zs], y_s.at[dy * 4 + zs], kv_r.at[dy * 4 + 4 + zs], grp, ctx + 4
        )

    @pl.when(y < 7)
    def _():
        forward(0, z).start()

    for i in range(3):
        copy(kv.at[0, :, z], kv.at[0, :, z], z_s.at[i], kv_r.at[z], grp, row_ctx[i]).start()
    for i in (1, 2, 0):
        copy(qall.at[member], qall.at[member], q_s.at[i], q_r.at[i], quad_grp[i], ctx).start()

    ticks = [(1, 0), (0, 1), (0, 2), (0, 3)] + [(dy, i) for dy in range(1, 5) for i in range(4)][1:]

    def tick(count=1):
        for _ in range(count):
            if not ticks:
                return
            dy, i = ticks.pop(0)
            zs = (z + i) % 4

            @pl.when(y >= dy)
            def _():
                arrived(kv.at[dy, :, zs], kv_r.at[dy * 4 + zs])

                if dy < 4:

                    @pl.when(y < 7)
                    def _():
                        forward(dy, zs).start()

    def tick_through(dy):
        while any(t[0] <= dy for t in ticks):
            tick()

    first = ctx * TOK
    ends = [lengths_ref[0] * BLOCK]
    for i in range(1, 4):
        ends.append(ends[-1] + lengths_ref[i] * BLOCK)
    for load in loads[3:9]:
        load.wait()

    def prompt(pos):
        total = (pos >= ends[0]).astype(F32)
        for e in ends[1:]:
            total += (pos >= e).astype(F32)
        return total

    row_i = lax.broadcasted_iota(jnp.int32, (1, TOK), 1)
    col_i = lax.broadcasted_iota(jnp.int32, (TOK, 1), 0)
    pid_row = prompt(first + row_i)
    pid_col = prompt(first + col_i)
    pid_before = prompt(jnp.full((1, 1), first - 1, jnp.int32))
    pid_last = prompt(jnp.full((1, 1), first + TOK - 1, jnp.int32))

    ii = lax.broadcasted_iota(jnp.int32, (TOK, TOK), 0)
    jj = lax.broadcasted_iota(jnp.int32, (TOK, TOK), 1)
    lower = (jj <= ii) & (pid_col == pid_row)
    strict = jj < ii

    d0 = decay_ref[...]
    d_hi = d0.astype(BF16)
    rest = d0 - d_hi.astype(F32)
    d_mid = rest.astype(BF16)
    d_lo = (rest - d_mid.astype(F32)).astype(BF16)
    upper_ones = (ii <= jj).astype(F32).astype(BF16)
    pieces = jnp.concatenate([d_hi.astype(F32), d_mid.astype(F32), d_lo.astype(F32), jnp.zeros((10, TOK), F32)], axis=0)
    sums = dot(pieces.astype(BF16), upper_ones)
    cum = sums[0:2] + sums[2:4] + sums[4:6]

    kf = dk_ref[...].astype(F32)
    qf = dq_ref[...].astype(F32)
    rk_col = lax.rsqrt(jnp.sum(kf * kf, axis=1, keepdims=True) + EPS)
    rq_col = lax.rsqrt(jnp.sum(qf * qf, axis=1, keepdims=True) + EPS)
    rk_row = jnp.broadcast_to(rk_col, (TOK, DHD)).T[0:1]
    packed = jnp.concatenate([cum, beta_ref[...], jnp.zeros((DHD - 4, TOK), F32)], axis=0).T
    kk = dot(dk_ref[...], dk_ref[...], NT) * rk_col * rk_row
    qk = dot(dq_ref[...], dk_ref[...], NT) * rq_col * rk_row

    decays, lows = [], []
    for h in range(2):
        diff = packed[:, h : h + 1] - cum[h : h + 1]
        decay = jnp.where(lower, jnp.exp(jnp.where(lower, diff, 0.0)), 0.0)
        decays.append(decay)
        lows.append(jnp.where(strict, packed[:, 2 + h : 3 + h] * decay * kk, 0.0))

    eye = (ii == jj).astype(F32)
    inverses = None
    size = 1
    while size < TOK:
        cross = (ii // (2 * size) == jj // (2 * size)) & (ii // size != jj // size)
        if size == 1:
            inverses = [eye - jnp.where(cross, low, 0.0) for low in lows]
        else:
            parts = [split(t) for t in inverses]
            inner = [dot3(split(jnp.where(cross, low, 0.0)), t) for low, t in zip(lows, parts)]
            inverses = [t - dot3(tp, split(m)) for t, tp, m in zip(inverses, parts, inner)]
            if size == 128:
                tick()
        size *= 2

    def unpack(message):
        gamma = jnp.sum(message[2 * DHD :].astype(F32), axis=0, keepdims=True)
        return message[0:DHD], message[DHD : 2 * DHD], gamma

    def apply_map(full, state_t, offset_t):
        g, _, gamma = full
        return gamma * state_t.astype(F32) - dot(state_t, g, NT) + offset_t.astype(F32)

    def compose(after, before):
        g2, o2, y2 = after
        g1, o1, y1 = before
        g = y2 * g1.astype(F32) + y1 * g2.astype(F32) - dot(g2, g1)
        return g, apply_map(after, o1, o2), y2 * y1

    def pack(step, h, g, o, gamma):
        g_hi = gamma.astype(BF16).astype(F32)
        csend[step, h, 0:DHD] = g.astype(BF16)
        csend[step, h, DHD : 2 * DHD] = o.astype(BF16)
        csend[step, h, 2 * DHD :] = jnp.where(sub == 0, g_hi, jnp.where(sub == 1, gamma - g_hi, 0.0)).astype(BF16)

    k_raw = dk_ref[...]
    k_t = kf.T.astype(BF16)
    sub = lax.broadcasted_iota(jnp.int32, (16, DHD), 0)
    later = []
    for h in range(2):
        alive_row = (pid_row == pid_before).astype(F32)
        alive_col = (pid_col == pid_before).astype(F32)
        growth_row = jnp.exp(cum[h : h + 1]) * alive_row
        growth_col = jnp.exp(packed[:, h : h + 1]) * alive_col
        beta_row = beta_ref[h : h + 1, :]
        u = dot2(split(inverses[h] * beta_row), dv_ref[:, h * DHD : (h + 1) * DHD])
        w = dot2(split(inverses[h] * (beta_row * growth_row * rk_row)), k_raw)
        wu = jnp.concatenate([w, u], axis=1)
        last = cum[h : h + 1, TOK - 1 : TOK]
        tail = jnp.where(pid_col == pid_last, jnp.exp(last - packed[:, h : h + 1]), 0.0) * rk_col
        tw = split(w * tail)
        maps = dot(k_t, tw[0]) + dot(k_t, tw[1])
        offsets_t = dot2(split((u * tail).T), k_raw)
        gamma = jnp.broadcast_to(growth_row[:, TOK - 1 : TOK], (1, DHD))
        pack(0, h, maps, offsets_t, gamma)
        later.append((wu, growth_col))

    def z_exchange(step):
        peer = y * 4 + (z + 1 - 2 * (z % 2) if step == 0 else (z + 2) % 4)
        return copy(csend.at[step], crecv.at[step], c_s.at[step], c_r.at[step], grp, peer)

    z_exchange(0).start()
    for h, (wu, growth_col) in enumerate(later):
        tick()
        pw = dot3(split(qk * decays[h]), split(wu))
        eff[h, :, :DHD] = (growth_col * rq_col) * qf - pw[:, :DHD]
        eff[h, :, DHD:] = pw[:, DHD:]

    def fold(step, recv_is_later):
        arrived(crecv.at[step], c_r.at[step])
        for first_later in (True, False):

            @pl.when(recv_is_later if first_later else jnp.logical_not(recv_is_later))
            def _():
                for h in range(2):
                    pair = unpack(crecv[step, h]), unpack(csend[step, h])
                    pack(step + 1, h, *compose(*(pair if first_later else pair[::-1])))

    quarter = pl.ds(pl.multiple_of(z * QUARTER, QUARTER), QUARTER)

    def row_hop(k):
        return copy(tsend.at[k], trecv.at[k], h_s.at[k], h_r.at[k], grp, ctx + 4)

    def hop_start(k):
        @pl.when(y < 7)
        def _():
            for h in range(2):
                offset = csend[2, h, pl.ds(pl.multiple_of(DHD + z * QUARTER, QUARTER), QUARTER)]
                if k == 0:
                    tsend[k, h] = offset
                else:
                    tsend[k, h] = apply_map(unpack(csend[2, h]), trecv[k - 1, h], offset).astype(BF16)
            row_hop(k).start()

    def hop_wait(k):
        @pl.when(y >= 1)
        def _():
            arrived(trecv.at[k], h_r.at[k])

        if k < 3:

            @pl.when(y < 1)
            def _():
                trecv[k] = jnp.zeros((2, QUARTER, DHD), BF16)

    def share(d):
        part = tall.at[:, quarter]
        return copy(part, part, g_s.at[d], g_r.at[d], grp, row_ctx[d])

    def share_start():
        @pl.when(y >= 1)
        def _():
            tall[:, quarter] = trecv[3]

        @pl.when(y < 1)
        def _():
            tall[:, quarter] = jnp.zeros((2, QUARTER, DHD), BF16)

        for d in range(3):
            share(d).start()

    def share_wait():
        for d in range(3):
            theirs = pl.ds(pl.multiple_of((z + 3 - d) % 4 * QUARTER, QUARTER), QUARTER)
            arrived(tall.at[:, theirs], g_r.at[d])
        state[...] = tall[...]
        for step, wanted in ((1, z >= 2), (0, z % 2 == 1)):

            @pl.when(wanted)
            def _():
                for h in range(2):
                    full = unpack(crecv[step, h])
                    state[h] = apply_map(full, state[h], full[1]).astype(BF16)

    quad_ready = [False]

    def attend(dy):
        tick_through(dy)
        if not quad_ready[0]:
            quad_ready[0] = True
            for i in range(3):
                arrived(qall.at[quad_member[i]], q_r.at[i])

        @pl.when(y >= dy)
        def _():
            key_pos = ((y - dy) * 4 + col_i // PIECE) * TOK + member * PIECE + col_i % PIECE
            keep = (key_pos <= first + row_i) & (prompt(key_pos) == pid_row)
            bias = jnp.where(keep, 0.0, MASKED)
            keys = kv[dy, 0].reshape(TOK, HD)
            vals_t = kv[dy, 1].reshape(TOK, HD).T
            for hh in range(4):
                s = dot(keys, qall[hh], NT) + bias
                top = jnp.max(s, axis=0, keepdims=True)
                if dy == 0:
                    new = jnp.maximum(top, START_MAX)
                    p = jnp.exp(s - new)
                    stat[hh, 1:2] = jnp.sum(p, axis=0, keepdims=True)
                    acc[hh] = dot(vals_t, p.astype(BF16))
                else:
                    old = stat[hh, 0:1]
                    new = jnp.maximum(old, top)
                    scale = jnp.exp(old - new)
                    p = jnp.exp(s - new)
                    stat[hh, 1:2] = stat[hh, 1:2] * scale + jnp.sum(p, axis=0, keepdims=True)
                    acc[hh] = acc[hh] * scale + dot(vals_t, p.astype(BF16))
                stat[hh, 0:1] = new

    tick()
    fold(0, z % 2 == 0)
    z_exchange(1).start()
    attend(0)
    tick(3)
    fold(1, z < 2)
    hop_start(0)
    tick(2)
    attend(1)
    hop_wait(0)
    hop_start(1)
    tick(2)
    attend(2)
    hop_wait(1)
    hop_start(2)
    tick(4)
    hop_wait(2)
    hop_start(3)
    attend(3)
    hop_wait(3)
    share_start()
    attend(4)

    def partial(i):
        return accs.at[i], accr.at[i], a_s.at[i], a_r.at[i], (xn_grp if i == 2 else sib_grp), ctx

    def partial_stats(i):
        return stats.at[i], statr.at[i], t_s.at[i], t_r.at[i], (xn_grp if i == 2 else sib_grp), ctx

    for i, m in ((1, quad_member[2]), (0, quad_member[0])):
        accs[i] = acc[m].astype(BF16)
        stats[i] = stat[m]
        copy(*partial_stats(i)).start()
        copy(*partial(i)).start()

    def project(p, heads, w_ref):
        for b in range(8):
            part = dot(heads, w_ref[:, b * 256 : (b + 1) * 256]).astype(BF16)
            pbuf[p, 0, b] = part[:, :DHD]
            pbuf[p, 1, b] = part[:, DHD:]
            i = p * 8 + b
            copy(pbuf.at[p, 1 - c, b], r1.at[p, b], s1_s.at[i], s1_r.at[i], sib_grp, ctx).start()

    half = [pl.ds(0, TOK // 2), pl.ds(TOK // 2, TOK // 2)]
    step1_grp, step2_grp = [xn_grp, xm_grp], [xm_grp, xn_grp]
    step1_x, step2_x = [xn, xm], [xm, xn]

    def pair_half(p, b, a):
        return pbuf[p, c, b, half[a]].astype(F32) + r1[p, b, half[a]].astype(F32)

    def copy_x1(p, a):
        i = p * 2 + a
        return copy(s2.at[p, a], r2.at[p, a], s2_s.at[i], s2_r.at[i], step1_grp[a], ctx)

    def copy_x2(p, a):
        i = 4 + p * 2 + a
        return copy(s4.at[p, a], r4.at[p, a], s2_s.at[i], s2_r.at[i], step2_grp[a], ctx)

    def across_x1(p):
        for b in range(8):
            arrived(r1.at[p, b], s1_r.at[p * 8 + b])
        for a in range(2):
            for e in range(2):
                s2[p, a, 0, e] = pair_half(p, step1_x[a] * 2 + e, a).astype(BF16)
                s2[p, a, 1, e] = pair_half(p, xo * 2 + e, a).astype(BF16)
            copy_x1(p, a).start()

    def across_x2(p):
        for a in range(2):
            arrived(r2.at[p, a], s2_r.at[p * 2 + a])
            for e in range(2):
                s4[p, a, e] = (pair_half(p, step2_x[a] * 2 + e, a) + r2[p, a, 1, e].astype(F32)).astype(BF16)
            copy_x2(p, a).start()

    def across_z(p):
        near = []
        for a in range(2):
            arrived(r4.at[p, a], s2_r.at[4 + p * 2 + a])
            far = pair_half(p, x * 2 + 1 - zh, a) + r2[p, a, 0, 1 - zh].astype(F32) + r4[p, a, 1 - zh].astype(F32)
            s3[p, half[a]] = far.astype(BF16)
            near.append(pair_half(p, x * 2 + zh, a) + r2[p, a, 0, zh].astype(F32) + r4[p, a, zh].astype(F32))
        copy(s3.at[p], r3.at[p], s3_s.at[p], s3_r.at[p], z_grp, ctx).start()
        return jnp.concatenate(near, axis=0)

    def finish(p, near, o_ref):
        arrived(r3.at[p], s3_r.at[p])
        o_ref[...] = (near + r3[p].astype(F32)).astype(BF16)

    for load in (loads[9], loads[11]):
        load.wait()
    share_wait()
    heads = []
    for h in range(2):
        e_hi, e_lo = split(eff[h, :, :DHD])
        core = dot(e_hi, state[h], NT) + dot(e_lo, state[h], NT) + eff[h, :, DHD:]
        squares = jnp.mean(core * core, axis=1, keepdims=True)
        gate = dgate_ref[:, h * DHD : (h + 1) * DHD].astype(F32)
        normed = core * lax.rsqrt(squares + EPS) * gain_ref[...]
        heads.append((normed * gate * jax.nn.sigmoid(gate)).astype(BF16))
    project(1, jnp.concatenate(heads, axis=1), wd_ref)
    def joined(accs_, stats_):
        top = stats_[0][0:1]
        for st in stats_[1:]:
            top = jnp.maximum(top, st[0:1])
        mixed, total = 0.0, 0.0
        for ac, st in zip(accs_, stats_):
            scale = jnp.exp(st[0:1] - top)
            mixed += ac.astype(F32) * scale
            total += st[1:2] * scale
        return mixed, top, total

    for i in (1, 0):
        arrived(statr.at[i], t_r.at[i])
        arrived(accr.at[i], a_r.at[i])
    for i, m in ((2, quad_member[1]), (3, member)):
        mixed, top, total = joined([acc[m], accr[3 - i]], [stat[m], statr[3 - i]])
        if i == 2:
            accs[i] = mixed.astype(BF16)
            stats[i, 0:1] = top
            stats[i, 1:2] = total
            copy(*partial_stats(i)).start()
            copy(*partial(i)).start()
        else:
            acc[m] = mixed
            stat[m, 0:1] = top
            stat[m, 1:2] = total
    across_x1(1)
    for load in (loads[10], loads[12]):
        load.wait()
    arrived(statr.at[2], t_r.at[2])
    arrived(accr.at[2], a_r.at[2])
    mixed, _, total = joined([acc[member], accr[2]], [stat[member], statr[2]])
    core_out = (mixed / total).T
    attn_heads = (core_out * jax.nn.sigmoid(agate_ref[...].astype(F32))).astype(BF16)
    project(0, attn_heads, wa_ref)
    across_x2(1)
    across_x1(0)
    near_d = across_z(1)
    across_x2(0)
    finish(1, near_d, od_ref)
    near_a = across_z(0)
    finish(0, near_a, oa_ref)

    for i in range(3):
        copy(kv.at[0, :, z], kv.at[0, :, z], z_s.at[i], kv_r.at[z], grp, row_ctx[i]).wait_send()
        copy(qall.at[member], qall.at[member], q_s.at[i], q_r.at[i], quad_grp[i], ctx).wait_send()
        copy(*partial_stats(i)).wait_send()
        copy(*partial(i)).wait_send()
    for dy in range(4):

        @pl.when((y >= dy) & (y < 7))
        def _():
            for zs in range(4):
                forward(dy, zs).wait_send()

    for step in range(2):
        z_exchange(step).wait_send()
    for d in range(3):
        share(d).wait_send()

    @pl.when(y < 7)
    def _():
        for k in range(4):
            row_hop(k).wait_send()

    for p in range(2):
        for b in range(8):
            i = p * 8 + b
            copy(pbuf.at[p, 1 - c, b], r1.at[p, b], s1_s.at[i], s1_r.at[i], sib_grp, ctx).wait_send()
        for a in range(2):
            copy_x1(p, a).wait_send()
            copy_x2(p, a).wait_send()
        copy(s3.at[p], r3.at[p], s3_s.at[p], s3_r.at[p], z_grp, ctx).wait_send()


def local(
    queries,
    keys,
    values,
    attn_gate,
    delta_query,
    delta_key,
    delta_value,
    delta_gate,
    decay_log,
    beta,
    norm_gain,
    attn_out_weight,
    delta_out_weight,
    doc_lengths,
):
    vmem = pl.BlockSpec(memory_space=pltpu.VMEM)
    anywhere = pl.BlockSpec(memory_space=pltpu.HBM)
    dma = lambda n: pltpu.SemaphoreType.DMA((n,))
    out = jax.ShapeDtypeStruct((TOK, DHD), BF16)
    return pl.pallas_call(
        kernel,
        out_shape=(out, out),
        in_specs=[pl.BlockSpec(memory_space=pltpu.SMEM)] + [anywhere] * 13,
        out_specs=(vmem, vmem),
        scratch_shapes=[
            pltpu.VMEM((TOK, HD), BF16),
            pltpu.VMEM((TOK, HD), BF16),
            pltpu.VMEM((TOK, DHD), BF16),
            pltpu.VMEM((TOK, DHD), BF16),
            pltpu.VMEM((TOK, 2 * DHD), BF16),
            pltpu.VMEM((TOK, 2 * DHD), BF16),
            pltpu.VMEM((2, TOK), F32),
            pltpu.VMEM((2, TOK), F32),
            pltpu.VMEM((1, DHD), F32),
            pltpu.VMEM((256, 2048), BF16),
            pltpu.VMEM((256, 2048), BF16),
            pltpu.VMEM((4, TOK, HD), BF16),
            pltpu.VMEM((5, 2, 4, PIECE, HD), BF16),
            pltpu.VMEM((4, HD, TOK), F32),
            pltpu.VMEM((4, 8, TOK), F32),
            pltpu.VMEM((3, HD, TOK), BF16),
            pltpu.VMEM((3, HD, TOK), BF16),
            pltpu.VMEM((3, 8, TOK), F32),
            pltpu.VMEM((3, 8, TOK), F32),
            pltpu.VMEM((3, 2, MSG, DHD), BF16),
            pltpu.VMEM((2, 2, MSG, DHD), BF16),
            pltpu.VMEM((4, 2, QUARTER, DHD), BF16),
            pltpu.VMEM((4, 2, QUARTER, DHD), BF16),
            pltpu.VMEM((2, DHD, DHD), BF16),
            pltpu.VMEM((2, DHD, DHD), BF16),
            pltpu.VMEM((2, TOK, 2 * DHD), F32),
            pltpu.VMEM((2, 2, 8, TOK, DHD), BF16),
            pltpu.VMEM((2, 8, TOK, DHD), BF16),
            pltpu.VMEM((2, 2, 2, 2, TOK // 2, DHD), BF16),
            pltpu.VMEM((2, 2, 2, 2, TOK // 2, DHD), BF16),
            pltpu.VMEM((2, 2, 2, TOK // 2, DHD), BF16),
            pltpu.VMEM((2, 2, 2, TOK // 2, DHD), BF16),
            pltpu.VMEM((2, TOK, DHD), BF16),
            pltpu.VMEM((2, TOK, DHD), BF16),
            dma(13),
            dma(3),
            dma(3),
            dma(3),
            dma(16),
            dma(20),
            dma(2),
            dma(2),
            dma(4),
            dma(4),
            dma(3),
            dma(3),
            dma(3),
            dma(3),
            dma(3),
            dma(3),
            dma(16),
            dma(16),
            dma(8),
            dma(8),
            dma(2),
            dma(2),
        ],
        compiler_params=pltpu.CompilerParams(
            collective_id=0, has_side_effects=True, vmem_limit_bytes=64 * 1024 * 1024
        ),
        cost_estimate=pl.CostEstimate(flops=4 * 10**9, bytes_accessed=6 * 10**6, transcendentals=2 * 10**6),
    )(
        doc_lengths,
        queries,
        keys,
        values,
        attn_gate,
        delta_query,
        delta_key,
        delta_value,
        delta_gate,
        decay_log,
        beta,
        norm_gain.reshape(1, DHD),
        attn_out_weight,
        delta_out_weight,
    )


def solution(mesh):
    placed = (
        P("ctx", "grp"),
        P("ctx", None),
        P("ctx", None),
        P("ctx", "grp"),
        P("ctx", "grp"),
        P("ctx", "grp"),
        P("ctx", "grp"),
        P("ctx", "grp"),
        P("grp", "ctx"),
        P("grp", "ctx"),
        P(),
        P("grp", None),
        P("grp", None),
        P(),
    )
    return jax.shard_map(
        local,
        mesh=mesh,
        in_specs=placed,
        out_specs=(P("ctx", "grp"), P("ctx", "grp")),
        check_vma=False,
    )
```

```python
import functools

import jax
import jax.numpy as jnp
from jax import lax
from jax.experimental import pallas as pl
from jax.experimental.pallas import tpu as pltpu
from jax.sharding import PartitionSpec as P

MESH = pl.DeviceIdType.MESH
F32 = jnp.float32
BF16 = jnp.bfloat16

HEADS = 16
HD = 256
KVH = 2
DHD = 128
BLOCK = 64
TOK = 256
PIECE = 64
QUARTER = DHD // 4
MSG = 2 * DHD + 16

EPS = 1e-06
MASKED = -2e30
START_MAX = -1e30

NT = (((1,), (1,)), ((), ()))
NN = (((1,), (0,)), ((), ()))


def dot(a, b, dims=NN):
    return lax.dot_general(a, b, dims, preferred_element_type=F32)


def split(x):
    high = x.astype(BF16)
    return high, (x - high.astype(F32)).astype(BF16)


def dot3(a, b):
    ah, al = a
    bh, bl = b
    return dot(ah, bh) + (dot(ah, bl) + dot(al, bh))


def dot2(a, b):
    return dot(a[0], b) + dot(a[1], b)


def kernel(
    lengths_ref,
    q_hbm,
    k_hbm,
    v_hbm,
    agate_hbm,
    dq_hbm,
    dk_hbm,
    dv_hbm,
    dgate_hbm,
    decay_hbm,
    beta_hbm,
    gain_hbm,
    wa_hbm,
    wd_hbm,
    oa_ref,
    od_ref,
    q_ref,
    agate_ref,
    dq_ref,
    dk_ref,
    dv_ref,
    dgate_ref,
    decay_ref,
    beta_ref,
    gain_ref,
    wa_ref,
    wd_ref,
    qall,
    kv,
    acc,
    stat,
    accs,
    accr,
    stats,
    statr,
    csend,
    crecv,
    tsend,
    trecv,
    tall,
    state,
    eff,
    pbuf,
    r1,
    s2,
    r2,
    s4,
    r4,
    s3,
    r3,
    w_sem,
    q_s,
    q_r,
    z_s,
    y_s,
    kv_r,
    c_s,
    c_r,
    h_s,
    h_r,
    g_s,
    g_r,
    a_s,
    a_r,
    t_s,
    t_r,
    s1_s,
    s1_r,
    s2_s,
    s2_r,
    s3_s,
    s3_r,
):
    grp = lax.axis_index("grp")
    ctx = lax.axis_index("ctx")
    x, zh, c = grp // 4, (grp // 2) % 2, grp % 2
    y, z = ctx // 4, ctx % 4
    xb = x % 2
    kvh = x // 2
    member = xb * 2 + c

    def grp_of(x_, zh_, c_):
        return x_ * 4 + zh_ * 2 + c_

    xn = x + 1 - 2 * xb
    quad = [(x, 1 - c), (xn, c), (xn, 1 - c)]
    quad_grp = [grp_of(a, zh, b) for a, b in quad]
    quad_member = [(a % 2) * 2 + b for a, b in quad]
    z_grp = grp_of(x, 1 - zh, c)
    sib_grp, xn_grp = quad_grp[0], quad_grp[1]
    xm = (x + 3 + 2 * xb) % 4
    xo = (x + 2) % 4
    xm_grp = grp_of(xm, zh, c)
    row_ctx = [y * 4 + (z + d) % 4 for d in (1, 2, 3)]

    def copy(src, dst, send, recv, g, r):
        return pltpu.make_async_remote_copy(
            src_ref=src,
            dst_ref=dst,
            send_sem=send,
            recv_sem=recv,
            device_id={"grp": g, "ctx": r},
            device_id_type=MESH,
        )

    def arrived(dst, sem):
        pltpu.make_async_copy(dst, dst, sem).wait()

    sends = []

    barrier = pltpu.get_barrier_semaphore()
    peers = [(g, ctx) for g in quad_grp + [xm_grp, z_grp]]
    peers += [(grp, r) for r in row_ctx]
    peers += [(grp, (ctx + d) % 32) for d in (4, 28)]
    for g, r in peers:
        pl.semaphore_signal(barrier, inc=1, device_id={"grp": g, "ctx": r}, device_id_type=MESH)

    rows = pl.ds(pl.multiple_of(member * PIECE, PIECE), PIECE)
    cols = pl.ds(pl.multiple_of(kvh * HD, HD), HD)
    loads = [
        pltpu.make_async_copy(src, dst, w_sem.at[i])
        for i, (src, dst) in enumerate(
            [
                (k_hbm.at[rows, cols], kv.at[0, 0, z]),
                (v_hbm.at[rows, cols], kv.at[0, 1, z]),
                (q_hbm, q_ref),
                (dk_hbm, dk_ref),
                (dq_hbm, dq_ref),
                (decay_hbm, decay_ref),
                (beta_hbm, beta_ref),
                (dv_hbm, dv_ref),
                (gain_hbm, gain_ref),
                (dgate_hbm, dgate_ref),
                (agate_hbm, agate_ref),
                (wd_hbm, wd_ref),
                (wa_hbm, wa_ref),
            ]
        )
    ]
    for load in loads:
        load.start()
    for load in loads[:3]:
        load.wait()
    qall[member] = q_ref[...] * jnp.asarray(HD ** (-0.5), BF16)
    pl.semaphore_wait(barrier, len(peers))

    def forward(dy, zs):
        return copy(
            kv.at[dy, :, zs], kv.at[dy + 1, :, zs], y_s.at[dy * 4 + zs], kv_r.at[dy * 4 + 4 + zs], grp, ctx + 4
        )

    @pl.when(y < 7)
    def _():
        forward(0, z).start()

    for i in range(3):
        copy(kv.at[0, :, z], kv.at[0, :, z], z_s.at[i], kv_r.at[z], grp, row_ctx[i]).start()
    for i in (1, 2, 0):
        copy(qall.at[member], qall.at[member], q_s.at[i], q_r.at[i], quad_grp[i], ctx).start()

    ticks = [(0, 1), (1, 0), (0, 2), (0, 3)] + [(dy, i) for dy in range(1, 5) for i in range(4)][1:]

    def tick(count=1):
        for _ in range(count):
            if not ticks:
                return
            dy, i = ticks.pop(0)
            zs = (z + 4 - i) % 4

            @pl.when(y >= dy)
            def _():
                arrived(kv.at[dy, :, zs], kv_r.at[dy * 4 + zs])

                if dy < 4:

                    @pl.when(y < 7)
                    def _():
                        forward(dy, zs).start()

    def tick_through(dy):
        while any(t[0] <= dy for t in ticks):
            tick()

    first = ctx * TOK
    ends = [lengths_ref[0] * BLOCK]
    for i in range(1, 4):
        ends.append(ends[-1] + lengths_ref[i] * BLOCK)
    for load in loads[3:9]:
        load.wait()

    def prompt(pos):
        total = (pos >= ends[0]).astype(F32)
        for e in ends[1:]:
            total += (pos >= e).astype(F32)
        return total

    row_i = lax.broadcasted_iota(jnp.int32, (1, TOK), 1)
    col_i = lax.broadcasted_iota(jnp.int32, (TOK, 1), 0)
    pid_row = prompt(first + row_i)
    pid_col = prompt(first + col_i)
    pid_before = prompt(jnp.full((1, 1), first - 1, jnp.int32))
    pid_last = prompt(jnp.full((1, 1), first + TOK - 1, jnp.int32))

    ii = lax.broadcasted_iota(jnp.int32, (TOK, TOK), 0)
    jj = lax.broadcasted_iota(jnp.int32, (TOK, TOK), 1)
    lower = (jj <= ii) & (pid_col == pid_row)
    strict = jj < ii

    d0 = decay_ref[...]
    d_hi = d0.astype(BF16)
    rest = d0 - d_hi.astype(F32)
    d_mid = rest.astype(BF16)
    d_lo = (rest - d_mid.astype(F32)).astype(BF16)
    upper_ones = (ii <= jj).astype(F32).astype(BF16)
    pieces = jnp.concatenate([d_hi.astype(F32), d_mid.astype(F32), d_lo.astype(F32), jnp.zeros((10, TOK), F32)], axis=0)
    sums = dot(pieces.astype(BF16), upper_ones)
    cum = sums[0:2] + sums[2:4] + sums[4:6]

    kf = dk_ref[...].astype(F32)
    qf = dq_ref[...].astype(F32)
    rk_col = lax.rsqrt(jnp.sum(kf * kf, axis=1, keepdims=True) + EPS)
    rq_col = lax.rsqrt(jnp.sum(qf * qf, axis=1, keepdims=True) + EPS)
    rk_row = jnp.broadcast_to(rk_col, (TOK, DHD)).T[0:1]
    packed = jnp.concatenate([cum, beta_ref[...], jnp.zeros((DHD - 4, TOK), F32)], axis=0).T
    kk = dot(dk_ref[...], dk_ref[...], NT) * rk_col * rk_row
    qk = dot(dq_ref[...], dk_ref[...], NT) * rq_col * rk_row

    decays, lows = [], []
    for h in range(2):
        diff = packed[:, h : h + 1] - cum[h : h + 1]
        decay = jnp.where(lower, jnp.exp(jnp.where(lower, diff, 0.0)), 0.0)
        decays.append(decay)
        lows.append(jnp.where(strict, packed[:, 2 + h : 3 + h] * decay * kk, 0.0))

    eye = (ii == jj).astype(F32)
    inverses = None
    size = 1
    while size < TOK:
        cross = (ii // (2 * size) == jj // (2 * size)) & (ii // size != jj // size)
        if size == 1:
            inverses = [eye - jnp.where(cross, low, 0.0) for low in lows]
        else:
            parts = [split(t) for t in inverses]
            inner = [dot3(split(jnp.where(cross, low, 0.0)), t) for low, t in zip(lows, parts)]
            inverses = [t - dot3(tp, split(m)) for t, tp, m in zip(inverses, parts, inner)]
            if size >= 64:
                tick()
        size *= 2

    def unpack(message):
        gamma = jnp.sum(message[2 * DHD :].astype(F32), axis=0, keepdims=True)
        return message[0:DHD], message[DHD : 2 * DHD], gamma

    def apply_map(full, state_t, offset_t):
        g, _, gamma = full
        return gamma * state_t.astype(F32) - dot(state_t, g, NT) + offset_t.astype(F32)

    def compose(after, before):
        g2, o2, y2 = after
        g1, o1, y1 = before
        g = y2 * g1.astype(F32) + y1 * g2.astype(F32) - dot(g2, g1)
        return g, apply_map(after, o1, o2), y2 * y1

    def pack(step, h, g, o, gamma):
        g_hi = gamma.astype(BF16).astype(F32)
        csend[step, h, 0:DHD] = g.astype(BF16)
        csend[step, h, DHD : 2 * DHD] = o.astype(BF16)
        csend[step, h, 2 * DHD :] = jnp.where(sub == 0, g_hi, jnp.where(sub == 1, gamma - g_hi, 0.0)).astype(BF16)

    k_raw = dk_ref[...]
    k_t = kf.T.astype(BF16)
    sub = lax.broadcasted_iota(jnp.int32, (16, DHD), 0)
    later = []
    for h in range(2):
        alive_row = (pid_row == pid_before).astype(F32)
        alive_col = (pid_col == pid_before).astype(F32)
        growth_row = jnp.exp(cum[h : h + 1]) * alive_row
        growth_col = jnp.exp(packed[:, h : h + 1]) * alive_col
        beta_row = beta_ref[h : h + 1, :]
        u = dot2(split(inverses[h] * beta_row), dv_ref[:, h * DHD : (h + 1) * DHD])
        w = dot2(split(inverses[h] * (beta_row * growth_row * rk_row)), k_raw)
        wu = jnp.concatenate([w, u], axis=1)
        last = cum[h : h + 1, TOK - 1 : TOK]
        tail = jnp.where(pid_col == pid_last, jnp.exp(last - packed[:, h : h + 1]), 0.0) * rk_col
        tw = split(w * tail)
        maps = dot(k_t, tw[0]) + dot(k_t, tw[1])
        offsets_t = dot2(split((u * tail).T), k_raw)
        gamma = jnp.broadcast_to(growth_row[:, TOK - 1 : TOK], (1, DHD))
        pack(0, h, maps, offsets_t, gamma)
        later.append((wu, growth_col))

    def z_exchange(step):
        peer = y * 4 + (z + 1 - 2 * (z % 2) if step == 0 else (z + 2) % 4)
        return copy(csend.at[step], crecv.at[step], c_s.at[step], c_r.at[step], grp, peer)

    z_exchange(0).start()
    for h, (wu, growth_col) in enumerate(later):
        tick()
        pw = dot3(split(qk * decays[h]), split(wu))
        eff[h, :, :DHD] = (growth_col * rq_col) * qf - pw[:, :DHD]
        eff[h, :, DHD:] = pw[:, DHD:]

    def fold(step, recv_is_later):
        arrived(crecv.at[step], c_r.at[step])
        for first_later in (True, False):

            @pl.when(recv_is_later if first_later else jnp.logical_not(recv_is_later))
            def _():
                for h in range(2):
                    pair = unpack(crecv[step, h]), unpack(csend[step, h])
                    pack(step + 1, h, *compose(*(pair if first_later else pair[::-1])))

    quarter = pl.ds(pl.multiple_of(z * QUARTER, QUARTER), QUARTER)

    def row_hop(k):
        return copy(tsend.at[k], trecv.at[k], h_s.at[k], h_r.at[k], grp, ctx + 4)

    def hop_start(k):
        @pl.when(y < 7)
        def _():
            for h in range(2):
                offset = csend[2, h, pl.ds(pl.multiple_of(DHD + z * QUARTER, QUARTER), QUARTER)]
                if k == 0:
                    tsend[k, h] = offset
                else:
                    tsend[k, h] = apply_map(unpack(csend[2, h]), trecv[k - 1, h], offset).astype(BF16)
            row_hop(k).start()

    def hop_wait(k):
        @pl.when(y >= 1)
        def _():
            arrived(trecv.at[k], h_r.at[k])

        if k < 3:

            @pl.when(y < 1)
            def _():
                trecv[k] = jnp.zeros((2, QUARTER, DHD), BF16)

    def share(d):
        part = tall.at[:, quarter]
        return copy(part, part, g_s.at[d], g_r.at[d], grp, row_ctx[d])

    def share_start():
        @pl.when(y >= 1)
        def _():
            tall[:, quarter] = trecv[3]

        @pl.when(y < 1)
        def _():
            tall[:, quarter] = jnp.zeros((2, QUARTER, DHD), BF16)

        for d in range(3):
            share(d).start()

    def share_wait():
        for d in range(3):
            theirs = pl.ds(pl.multiple_of((z + 3 - d) % 4 * QUARTER, QUARTER), QUARTER)
            arrived(tall.at[:, theirs], g_r.at[d])
        state[...] = tall[...]
        for step, wanted in ((1, z >= 2), (0, z % 2 == 1)):

            @pl.when(wanted)
            def _():
                for h in range(2):
                    full = unpack(crecv[step, h])
                    state[h] = apply_map(full, state[h], full[1]).astype(BF16)

    quad_ready = [False]

    def attend(dy):
        tick_through(dy)
        if not quad_ready[0]:
            quad_ready[0] = True
            for i in range(3):
                arrived(qall.at[quad_member[i]], q_r.at[i])

        @pl.when(y >= dy)
        def _():
            key_pos = ((y - dy) * 4 + col_i // PIECE) * TOK + member * PIECE + col_i % PIECE
            keep = (key_pos <= first + row_i) & (prompt(key_pos) == pid_row)
            bias = jnp.where(keep, 0.0, MASKED)
            keys = kv[dy, 0].reshape(TOK, HD)
            vals_t = kv[dy, 1].reshape(TOK, HD).T
            for hh in range(4):
                s = dot(keys, qall[hh], NT) + bias
                top = jnp.max(s, axis=0, keepdims=True)
                if dy == 0:
                    new = jnp.maximum(top, START_MAX)
                    p = jnp.exp(s - new)
                    stat[hh, 1:2] = jnp.sum(p, axis=0, keepdims=True)
                    acc[hh] = dot(vals_t, p.astype(BF16))
                else:
                    old = stat[hh, 0:1]
                    new = jnp.maximum(old, top)
                    scale = jnp.exp(old - new)
                    p = jnp.exp(s - new)
                    stat[hh, 1:2] = stat[hh, 1:2] * scale + jnp.sum(p, axis=0, keepdims=True)
                    acc[hh] = acc[hh] * scale + dot(vals_t, p.astype(BF16))
                stat[hh, 0:1] = new

    tick()
    fold(0, z % 2 == 0)
    z_exchange(1).start()
    attend(0)
    tick(3)
    fold(1, z < 2)
    hop_start(0)
    tick(2)
    attend(1)
    hop_wait(0)
    hop_start(1)
    tick(2)
    hop_wait(1)
    hop_start(2)
    tick(2)
    attend(2)
    hop_wait(2)
    hop_start(3)
    tick(2)
    hop_wait(3)
    share_start()
    attend(3)
    attend(4)

    def partial(i):
        return accs.at[i], accr.at[i], a_s.at[i], a_r.at[i], (xn_grp if i == 2 else sib_grp), ctx

    def partial_stats(i):
        return stats.at[i], statr.at[i], t_s.at[i], t_r.at[i], (xn_grp if i == 2 else sib_grp), ctx

    for i, m in ((1, quad_member[2]), (0, quad_member[0])):
        accs[i] = acc[m].astype(BF16)
        stats[i] = stat[m]
        copy(*partial_stats(i)).start()
        copy(*partial(i)).start()

    def project(p, heads, w_ref):
        for b in range(8):
            part = dot(heads, w_ref[:, b * 256 : (b + 1) * 256]).astype(BF16)
            pbuf[p, 0, b] = part[:, :DHD]
            pbuf[p, 1, b] = part[:, DHD:]
            i = p * 8 + b
            copy(pbuf.at[p, 1 - c, b], r1.at[p, b], s1_s.at[i], s1_r.at[i], sib_grp, ctx).start()

    half = [pl.ds(0, TOK // 2), pl.ds(TOK // 2, TOK // 2)]
    step1_grp, step2_grp = [xn_grp, xm_grp], [xm_grp, xn_grp]
    step1_x, step2_x = [xn, xm], [xm, xn]

    def pair_half(p, b, a):
        return pbuf[p, c, b, half[a]].astype(F32) + r1[p, b, half[a]].astype(F32)

    def copy_x1(p, a):
        i = p * 2 + a
        return copy(s2.at[p, a], r2.at[p, a], s2_s.at[i], s2_r.at[i], step1_grp[a], ctx)

    def copy_x2(p, a):
        i = 4 + p * 2 + a
        return copy(s4.at[p, a], r4.at[p, a], s2_s.at[i], s2_r.at[i], step2_grp[a], ctx)

    def across_x1(p):
        for b in range(8):
            arrived(r1.at[p, b], s1_r.at[p * 8 + b])
        for a in range(2):
            for e in range(2):
                s2[p, a, 0, e] = pair_half(p, step1_x[a] * 2 + e, a).astype(BF16)
                s2[p, a, 1, e] = pair_half(p, xo * 2 + e, a).astype(BF16)
            copy_x1(p, a).start()

    def across_x2(p):
        for a in range(2):
            arrived(r2.at[p, a], s2_r.at[p * 2 + a])
            for e in range(2):
                s4[p, a, e] = (pair_half(p, step2_x[a] * 2 + e, a) + r2[p, a, 1, e].astype(F32)).astype(BF16)
            copy_x2(p, a).start()

    def across_z(p):
        near = []
        for a in range(2):
            arrived(r4.at[p, a], s2_r.at[4 + p * 2 + a])
            far = pair_half(p, x * 2 + 1 - zh, a) + r2[p, a, 0, 1 - zh].astype(F32) + r4[p, a, 1 - zh].astype(F32)
            s3[p, half[a]] = far.astype(BF16)
            near.append(pair_half(p, x * 2 + zh, a) + r2[p, a, 0, zh].astype(F32) + r4[p, a, zh].astype(F32))
        copy(s3.at[p], r3.at[p], s3_s.at[p], s3_r.at[p], z_grp, ctx).start()
        return jnp.concatenate(near, axis=0)

    def finish(p, near, o_ref):
        arrived(r3.at[p], s3_r.at[p])
        o_ref[...] = (near + r3[p].astype(F32)).astype(BF16)

    for load in (loads[9], loads[11]):
        load.wait()
    share_wait()
    heads = []
    for h in range(2):
        e_hi, e_lo = split(eff[h, :, :DHD])
        core = dot(e_hi, state[h], NT) + dot(e_lo, state[h], NT) + eff[h, :, DHD:]
        squares = jnp.mean(core * core, axis=1, keepdims=True)
        gate = dgate_ref[:, h * DHD : (h + 1) * DHD].astype(F32)
        normed = core * lax.rsqrt(squares + EPS) * gain_ref[...]
        heads.append((normed * gate * jax.nn.sigmoid(gate)).astype(BF16))
    def joined(accs_, stats_):
        top = stats_[0][0:1]
        for st in stats_[1:]:
            top = jnp.maximum(top, st[0:1])
        mixed, total = 0.0, 0.0
        for ac, st in zip(accs_, stats_):
            scale = jnp.exp(st[0:1] - top)
            mixed += ac.astype(F32) * scale
            total += st[1:2] * scale
        return mixed, top, total

    for i in (1, 0):
        arrived(statr.at[i], t_r.at[i])
        arrived(accr.at[i], a_r.at[i])
    for i, m in ((2, quad_member[1]), (3, member)):
        mixed, top, total = joined([acc[m], accr[3 - i]], [stat[m], statr[3 - i]])
        if i == 2:
            accs[i] = mixed.astype(BF16)
            stats[i, 0:1] = top
            stats[i, 1:2] = total
            copy(*partial_stats(i)).start()
            copy(*partial(i)).start()
        else:
            acc[m] = mixed
            stat[m, 0:1] = top
            stat[m, 1:2] = total
    project(1, jnp.concatenate(heads, axis=1), wd_ref)
    across_x1(1)
    for load in (loads[10], loads[12]):
        load.wait()
    arrived(statr.at[2], t_r.at[2])
    arrived(accr.at[2], a_r.at[2])
    mixed, _, total = joined([acc[member], accr[2]], [stat[member], statr[2]])
    core_out = (mixed / total).T
    attn_heads = (core_out * jax.nn.sigmoid(agate_ref[...].astype(F32))).astype(BF16)
    project(0, attn_heads, wa_ref)
    across_x2(1)
    across_x1(0)
    near_d = across_z(1)
    across_x2(0)
    finish(1, near_d, od_ref)
    near_a = across_z(0)
    finish(0, near_a, oa_ref)

    for i in range(3):
        copy(kv.at[0, :, z], kv.at[0, :, z], z_s.at[i], kv_r.at[z], grp, row_ctx[i]).wait_send()
        copy(qall.at[member], qall.at[member], q_s.at[i], q_r.at[i], quad_grp[i], ctx).wait_send()
        copy(*partial_stats(i)).wait_send()
        copy(*partial(i)).wait_send()
    for dy in range(4):

        @pl.when((y >= dy) & (y < 7))
        def _():
            for zs in range(4):
                forward(dy, zs).wait_send()

    for step in range(2):
        z_exchange(step).wait_send()
    for d in range(3):
        share(d).wait_send()

    @pl.when(y < 7)
    def _():
        for k in range(4):
            row_hop(k).wait_send()

    for p in range(2):
        for b in range(8):
            i = p * 8 + b
            copy(pbuf.at[p, 1 - c, b], r1.at[p, b], s1_s.at[i], s1_r.at[i], sib_grp, ctx).wait_send()
        for a in range(2):
            copy_x1(p, a).wait_send()
            copy_x2(p, a).wait_send()
        copy(s3.at[p], r3.at[p], s3_s.at[p], s3_r.at[p], z_grp, ctx).wait_send()


def local(
    queries,
    keys,
    values,
    attn_gate,
    delta_query,
    delta_key,
    delta_value,
    delta_gate,
    decay_log,
    beta,
    norm_gain,
    attn_out_weight,
    delta_out_weight,
    doc_lengths,
):
    vmem = pl.BlockSpec(memory_space=pltpu.VMEM)
    anywhere = pl.BlockSpec(memory_space=pltpu.HBM)
    dma = lambda n: pltpu.SemaphoreType.DMA((n,))
    out = jax.ShapeDtypeStruct((TOK, DHD), BF16)
    return pl.pallas_call(
        kernel,
        out_shape=(out, out),
        in_specs=[pl.BlockSpec(memory_space=pltpu.SMEM)] + [anywhere] * 13,
        out_specs=(vmem, vmem),
        scratch_shapes=[
            pltpu.VMEM((TOK, HD), BF16),
            pltpu.VMEM((TOK, HD), BF16),
            pltpu.VMEM((TOK, DHD), BF16),
            pltpu.VMEM((TOK, DHD), BF16),
            pltpu.VMEM((TOK, 2 * DHD), BF16),
            pltpu.VMEM((TOK, 2 * DHD), BF16),
            pltpu.VMEM((2, TOK), F32),
            pltpu.VMEM((2, TOK), F32),
            pltpu.VMEM((1, DHD), F32),
            pltpu.VMEM((256, 2048), BF16),
            pltpu.VMEM((256, 2048), BF16),
            pltpu.VMEM((4, TOK, HD), BF16),
            pltpu.VMEM((5, 2, 4, PIECE, HD), BF16),
            pltpu.VMEM((4, HD, TOK), F32),
            pltpu.VMEM((4, 8, TOK), F32),
            pltpu.VMEM((3, HD, TOK), BF16),
            pltpu.VMEM((3, HD, TOK), BF16),
            pltpu.VMEM((3, 8, TOK), F32),
            pltpu.VMEM((3, 8, TOK), F32),
            pltpu.VMEM((3, 2, MSG, DHD), BF16),
            pltpu.VMEM((2, 2, MSG, DHD), BF16),
            pltpu.VMEM((4, 2, QUARTER, DHD), BF16),
            pltpu.VMEM((4, 2, QUARTER, DHD), BF16),
            pltpu.VMEM((2, DHD, DHD), BF16),
            pltpu.VMEM((2, DHD, DHD), BF16),
            pltpu.VMEM((2, TOK, 2 * DHD), F32),
            pltpu.VMEM((2, 2, 8, TOK, DHD), BF16),
            pltpu.VMEM((2, 8, TOK, DHD), BF16),
            pltpu.VMEM((2, 2, 2, 2, TOK // 2, DHD), BF16),
            pltpu.VMEM((2, 2, 2, 2, TOK // 2, DHD), BF16),
            pltpu.VMEM((2, 2, 2, TOK // 2, DHD), BF16),
            pltpu.VMEM((2, 2, 2, TOK // 2, DHD), BF16),
            pltpu.VMEM((2, TOK, DHD), BF16),
            pltpu.VMEM((2, TOK, DHD), BF16),
            dma(13),
            dma(3),
            dma(3),
            dma(3),
            dma(16),
            dma(20),
            dma(2),
            dma(2),
            dma(4),
            dma(4),
            dma(3),
            dma(3),
            dma(3),
            dma(3),
            dma(3),
            dma(3),
            dma(16),
            dma(16),
            dma(8),
            dma(8),
            dma(2),
            dma(2),
        ],
        compiler_params=pltpu.CompilerParams(
            collective_id=0, has_side_effects=True, vmem_limit_bytes=64 * 1024 * 1024
        ),
        cost_estimate=pl.CostEstimate(flops=4 * 10**9, bytes_accessed=6 * 10**6, transcendentals=2 * 10**6),
    )(
        doc_lengths,
        queries,
        keys,
        values,
        attn_gate,
        delta_query,
        delta_key,
        delta_value,
        delta_gate,
        decay_log,
        beta,
        norm_gain.reshape(1, DHD),
        attn_out_weight,
        delta_out_weight,
    )


def solution(mesh):
    placed = (
        P("ctx", "grp"),
        P("ctx", None),
        P("ctx", None),
        P("ctx", "grp"),
        P("ctx", "grp"),
        P("ctx", "grp"),
        P("ctx", "grp"),
        P("ctx", "grp"),
        P("grp", "ctx"),
        P("grp", "ctx"),
        P(),
        P("grp", None),
        P("grp", None),
        P(),
    )
    return jax.shard_map(
        local,
        mesh=mesh,
        in_specs=placed,
        out_specs=(P("ctx", "grp"), P("ctx", "grp")),
        check_vma=False,
    )
```

```python
import functools

import jax
import jax.numpy as jnp
from jax import lax
from jax.experimental import pallas as pl
from jax.experimental.pallas import tpu as pltpu
from jax.sharding import PartitionSpec as P

MESH = pl.DeviceIdType.MESH
F32 = jnp.float32
BF16 = jnp.bfloat16

HEADS = 16
HD = 256
KVH = 2
DHD = 128
BLOCK = 64
TOK = 256
PIECE = 64
QUARTER = DHD // 4
MSG = 2 * DHD + 16

EPS = 1e-06
MASKED = -2e30
START_MAX = -1e30

NT = (((1,), (1,)), ((), ()))
NN = (((1,), (0,)), ((), ()))


def dot(a, b, dims=NN):
    return lax.dot_general(a, b, dims, preferred_element_type=F32)


def split(x):
    high = x.astype(BF16)
    return high, (x - high.astype(F32)).astype(BF16)


def dot3(a, b):
    ah, al = a
    bh, bl = b
    return dot(ah, bh) + (dot(ah, bl) + dot(al, bh))


def dot2(a, b):
    return dot(a[0], b) + dot(a[1], b)


def kernel(
    lengths_ref,
    q_hbm,
    k_hbm,
    v_hbm,
    agate_hbm,
    dq_hbm,
    dk_hbm,
    dv_hbm,
    dgate_hbm,
    decay_hbm,
    beta_hbm,
    gain_hbm,
    wa_hbm,
    wd_hbm,
    oa_ref,
    od_ref,
    q_ref,
    agate_ref,
    dq_ref,
    dk_ref,
    dv_ref,
    dgate_ref,
    decay_ref,
    beta_ref,
    gain_ref,
    wa_ref,
    wd_ref,
    qall,
    kv,
    acc,
    stat,
    accs,
    accr,
    stats,
    statr,
    csend,
    crecv,
    tsend,
    trecv,
    tall,
    state,
    eff,
    pbuf,
    r1,
    s2,
    r2,
    s4,
    r4,
    s3,
    r3,
    w_sem,
    q_s,
    q_r,
    z_s,
    y_s,
    kv_r,
    c_s,
    c_r,
    h_s,
    h_r,
    g_s,
    g_r,
    a_s,
    a_r,
    t_s,
    t_r,
    s1_s,
    s1_r,
    s2_s,
    s2_r,
    s3_s,
    s3_r,
):
    grp = lax.axis_index("grp")
    ctx = lax.axis_index("ctx")
    x, zh, c = grp // 4, (grp // 2) % 2, grp % 2
    y, z = ctx // 4, ctx % 4
    xb = x % 2
    kvh = x // 2
    member = xb * 2 + c

    def grp_of(x_, zh_, c_):
        return x_ * 4 + zh_ * 2 + c_

    xn = x + 1 - 2 * xb
    quad = [(x, 1 - c), (xn, c), (xn, 1 - c)]
    quad_grp = [grp_of(a, zh, b) for a, b in quad]
    quad_member = [(a % 2) * 2 + b for a, b in quad]
    z_grp = grp_of(x, 1 - zh, c)
    sib_grp, xn_grp = quad_grp[0], quad_grp[1]
    xm = (x + 3 + 2 * xb) % 4
    xo = (x + 2) % 4
    xm_grp = grp_of(xm, zh, c)
    row_ctx = [y * 4 + (z + d) % 4 for d in (1, 2, 3)]

    def copy(src, dst, send, recv, g, r):
        return pltpu.make_async_remote_copy(
            src_ref=src,
            dst_ref=dst,
            send_sem=send,
            recv_sem=recv,
            device_id={"grp": g, "ctx": r},
            device_id_type=MESH,
        )

    def arrived(dst, sem):
        pltpu.make_async_copy(dst, dst, sem).wait()

    sends = []

    barrier = pltpu.get_barrier_semaphore()
    peers = [(g, ctx) for g in quad_grp + [xm_grp, z_grp]]
    peers += [(grp, r) for r in row_ctx]
    peers += [(grp, (ctx + d) % 32) for d in (4, 28)]
    for g, r in peers:
        pl.semaphore_signal(barrier, inc=1, device_id={"grp": g, "ctx": r}, device_id_type=MESH)

    rows = pl.ds(pl.multiple_of(member * PIECE, PIECE), PIECE)
    cols = pl.ds(pl.multiple_of(kvh * HD, HD), HD)
    loads = [
        pltpu.make_async_copy(src, dst, w_sem.at[i])
        for i, (src, dst) in enumerate(
            [
                (k_hbm.at[rows, cols], kv.at[0, 0, z]),
                (v_hbm.at[rows, cols], kv.at[0, 1, z]),
                (q_hbm, q_ref),
                (dk_hbm, dk_ref),
                (dq_hbm, dq_ref),
                (decay_hbm, decay_ref),
                (beta_hbm, beta_ref),
                (dv_hbm, dv_ref),
                (gain_hbm, gain_ref),
                (dgate_hbm, dgate_ref),
                (agate_hbm, agate_ref),
                (wd_hbm, wd_ref),
                (wa_hbm, wa_ref),
            ]
        )
    ]
    for load in loads:
        load.start()
    for load in loads[:3]:
        load.wait()
    qall[member] = q_ref[...] * jnp.asarray(HD ** (-0.5), BF16)
    pl.semaphore_wait(barrier, len(peers))

    def forward(dy, zs):
        return copy(
            kv.at[dy, :, zs], kv.at[dy + 1, :, zs], y_s.at[dy * 4 + zs], kv_r.at[dy * 4 + 4 + zs], grp, ctx + 4
        )

    @pl.when(y < 7)
    def _():
        forward(0, z).start()

    for i in range(3):
        copy(kv.at[0, :, z], kv.at[0, :, z], z_s.at[i], kv_r.at[z], grp, row_ctx[i]).start()
    for i in (1, 2, 0):
        copy(qall.at[member], qall.at[member], q_s.at[i], q_r.at[i], quad_grp[i], ctx).start()

    ticks = [(0, 1), (1, 0), (0, 2), (0, 3)] + [(dy, i) for dy in range(1, 5) for i in range(4)][1:]

    def tick(count=1):
        for _ in range(count):
            if not ticks:
                return
            dy, i = ticks.pop(0)
            zs = (z + 4 - i) % 4

            @pl.when(y >= dy)
            def _():
                arrived(kv.at[dy, :, zs], kv_r.at[dy * 4 + zs])

                if dy < 4:

                    @pl.when(y < 7)
                    def _():
                        forward(dy, zs).start()

    def tick_through(dy):
        while any(t[0] <= dy for t in ticks):
            tick()

    first = ctx * TOK
    ends = [lengths_ref[0] * BLOCK]
    for i in range(1, 4):
        ends.append(ends[-1] + lengths_ref[i] * BLOCK)
    for load in loads[3:9]:
        load.wait()

    def prompt(pos):
        total = (pos >= ends[0]).astype(F32)
        for e in ends[1:]:
            total += (pos >= e).astype(F32)
        return total

    row_i = lax.broadcasted_iota(jnp.int32, (1, TOK), 1)
    col_i = lax.broadcasted_iota(jnp.int32, (TOK, 1), 0)
    pid_row = prompt(first + row_i)
    pid_col = prompt(first + col_i)
    pid_before = prompt(jnp.full((1, 1), first - 1, jnp.int32))
    pid_last = prompt(jnp.full((1, 1), first + TOK - 1, jnp.int32))

    ii = lax.broadcasted_iota(jnp.int32, (TOK, TOK), 0)
    jj = lax.broadcasted_iota(jnp.int32, (TOK, TOK), 1)
    lower = (jj <= ii) & (pid_col == pid_row)
    strict = jj < ii

    d0 = decay_ref[...]
    d_hi = d0.astype(BF16)
    rest = d0 - d_hi.astype(F32)
    d_mid = rest.astype(BF16)
    d_lo = (rest - d_mid.astype(F32)).astype(BF16)
    upper_ones = (ii <= jj).astype(F32).astype(BF16)
    pieces = jnp.concatenate([d_hi.astype(F32), d_mid.astype(F32), d_lo.astype(F32), jnp.zeros((10, TOK), F32)], axis=0)
    sums = dot(pieces.astype(BF16), upper_ones)
    cum = sums[0:2] + sums[2:4] + sums[4:6]

    kf = dk_ref[...].astype(F32)
    qf = dq_ref[...].astype(F32)
    rk_col = lax.rsqrt(jnp.sum(kf * kf, axis=1, keepdims=True) + EPS)
    rq_col = lax.rsqrt(jnp.sum(qf * qf, axis=1, keepdims=True) + EPS)
    rk_row = jnp.broadcast_to(rk_col, (TOK, DHD)).T[0:1]
    packed = jnp.concatenate([cum, beta_ref[...], jnp.zeros((DHD - 4, TOK), F32)], axis=0).T
    kk = dot(dk_ref[...], dk_ref[...], NT) * rk_col * rk_row
    qk = dot(dq_ref[...], dk_ref[...], NT) * rq_col * rk_row

    decays, lows = [], []
    for h in range(2):
        diff = packed[:, h : h + 1] - cum[h : h + 1]
        decay = jnp.where(lower, jnp.exp(jnp.where(lower, diff, 0.0)), 0.0)
        decays.append(decay)
        lows.append(jnp.where(strict, packed[:, 2 + h : 3 + h] * decay * kk, 0.0))

    eye = (ii == jj).astype(F32)
    inverses = None
    size = 1
    while size < TOK:
        cross = (ii // (2 * size) == jj // (2 * size)) & (ii // size != jj // size)
        if size == 1:
            inverses = [eye - jnp.where(cross, low, 0.0) for low in lows]
        elif size == TOK // 2:
            joined_up = []
            for low, t in zip(lows, inverses):
                above, below = t[:size, :size], t[size:, size:]
                inner = dot3(split(low[size:, :size]), split(above))
                corner = -dot3(split(below), split(inner))
                joined_up.append(jnp.concatenate([t[:size], jnp.concatenate([corner, below], axis=1)], axis=0))
            inverses = joined_up
            tick()
        else:
            parts = [split(t) for t in inverses]
            inner = [dot3(split(jnp.where(cross, low, 0.0)), t) for low, t in zip(lows, parts)]
            inverses = [t - dot3(tp, split(m)) for t, tp, m in zip(inverses, parts, inner)]
            if size >= 64:
                tick()
        size *= 2

    def unpack(message):
        gamma = jnp.sum(message[2 * DHD :].astype(F32), axis=0, keepdims=True)
        return message[0:DHD], message[DHD : 2 * DHD], gamma

    def apply_map(full, state_t, offset_t):
        g, _, gamma = full
        return gamma * state_t.astype(F32) - dot(state_t, g, NT) + offset_t.astype(F32)

    def compose(after, before):
        g2, o2, y2 = after
        g1, o1, y1 = before
        g = y2 * g1.astype(F32) + y1 * g2.astype(F32) - dot(g2, g1)
        return g, apply_map(after, o1, o2), y2 * y1

    def pack(step, h, g, o, gamma):
        g_hi = gamma.astype(BF16).astype(F32)
        csend[step, h, 0:DHD] = g.astype(BF16)
        csend[step, h, DHD : 2 * DHD] = o.astype(BF16)
        csend[step, h, 2 * DHD :] = jnp.where(sub == 0, g_hi, jnp.where(sub == 1, gamma - g_hi, 0.0)).astype(BF16)

    k_raw = dk_ref[...]
    k_t = kf.T.astype(BF16)
    sub = lax.broadcasted_iota(jnp.int32, (16, DHD), 0)
    later = []
    for h in range(2):
        alive_row = (pid_row == pid_before).astype(F32)
        alive_col = (pid_col == pid_before).astype(F32)
        growth_row = jnp.exp(cum[h : h + 1]) * alive_row
        growth_col = jnp.exp(packed[:, h : h + 1]) * alive_col
        beta_row = beta_ref[h : h + 1, :]
        u = dot2(split(inverses[h] * beta_row), dv_ref[:, h * DHD : (h + 1) * DHD])
        w = dot2(split(inverses[h] * (beta_row * growth_row * rk_row)), k_raw)
        wu = jnp.concatenate([w, u], axis=1)
        last = cum[h : h + 1, TOK - 1 : TOK]
        tail = jnp.where(pid_col == pid_last, jnp.exp(last - packed[:, h : h + 1]), 0.0) * rk_col
        tw = split(w * tail)
        maps = dot(k_t, tw[0]) + dot(k_t, tw[1])
        offsets_t = dot2(split((u * tail).T), k_raw)
        gamma = jnp.broadcast_to(growth_row[:, TOK - 1 : TOK], (1, DHD))
        pack(0, h, maps, offsets_t, gamma)
        later.append((wu, growth_col))

    def z_exchange(step):
        peer = y * 4 + (z + 1 - 2 * (z % 2) if step == 0 else (z + 2) % 4)
        return copy(csend.at[step], crecv.at[step], c_s.at[step], c_r.at[step], grp, peer)

    z_exchange(0).start()
    for h, (wu, growth_col) in enumerate(later):
        tick()
        pw = dot3(split(qk * decays[h]), split(wu))
        eff[h, :, :DHD] = (growth_col * rq_col) * qf - pw[:, :DHD]
        eff[h, :, DHD:] = pw[:, DHD:]

    def fold(step, recv_is_later):
        arrived(crecv.at[step], c_r.at[step])
        for first_later in (True, False):

            @pl.when(recv_is_later if first_later else jnp.logical_not(recv_is_later))
            def _():
                for h in range(2):
                    pair = unpack(crecv[step, h]), unpack(csend[step, h])
                    pack(step + 1, h, *compose(*(pair if first_later else pair[::-1])))

    quarter = pl.ds(pl.multiple_of(z * QUARTER, QUARTER), QUARTER)

    def row_hop(k):
        return copy(tsend.at[k], trecv.at[k], h_s.at[k], h_r.at[k], grp, ctx + 4)

    def hop_start(k):
        @pl.when(y < 7)
        def _():
            for h in range(2):
                offset = csend[2, h, pl.ds(pl.multiple_of(DHD + z * QUARTER, QUARTER), QUARTER)]
                if k == 0:
                    tsend[k, h] = offset
                else:
                    tsend[k, h] = apply_map(unpack(csend[2, h]), trecv[k - 1, h], offset).astype(BF16)
            row_hop(k).start()

    def hop_wait(k):
        @pl.when(y >= 1)
        def _():
            arrived(trecv.at[k], h_r.at[k])

        if k < 3:

            @pl.when(y < 1)
            def _():
                trecv[k] = jnp.zeros((2, QUARTER, DHD), BF16)

    def share(d):
        part = tall.at[:, quarter]
        return copy(part, part, g_s.at[d], g_r.at[d], grp, row_ctx[d])

    def share_start():
        @pl.when(y >= 1)
        def _():
            tall[:, quarter] = trecv[3]

        @pl.when(y < 1)
        def _():
            tall[:, quarter] = jnp.zeros((2, QUARTER, DHD), BF16)

        for d in range(3):
            share(d).start()

    def share_wait():
        for d in range(3):
            theirs = pl.ds(pl.multiple_of((z + 3 - d) % 4 * QUARTER, QUARTER), QUARTER)
            arrived(tall.at[:, theirs], g_r.at[d])
        state[...] = tall[...]
        for step, wanted in ((1, z >= 2), (0, z % 2 == 1)):

            @pl.when(wanted)
            def _():
                for h in range(2):
                    full = unpack(crecv[step, h])
                    state[h] = apply_map(full, state[h], full[1]).astype(BF16)

    quad_ready = [False]

    def attend(dy):
        tick_through(dy)
        if not quad_ready[0]:
            quad_ready[0] = True
            for i in range(3):
                arrived(qall.at[quad_member[i]], q_r.at[i])

        @pl.when(y >= dy)
        def _():
            key_pos = ((y - dy) * 4 + col_i // PIECE) * TOK + member * PIECE + col_i % PIECE
            keep = (key_pos <= first + row_i) & (prompt(key_pos) == pid_row)
            bias = jnp.where(keep, 0.0, MASKED)
            keys = kv[dy, 0].reshape(TOK, HD)
            vals_t = kv[dy, 1].reshape(TOK, HD).T
            for hh in range(4):
                s = dot(keys, qall[hh], NT) + bias
                top = jnp.max(s, axis=0, keepdims=True)
                if dy == 0:
                    new = jnp.maximum(top, START_MAX)
                    p = jnp.exp(s - new)
                    stat[hh, 1:2] = jnp.sum(p, axis=0, keepdims=True)
                    acc[hh] = dot(vals_t, p.astype(BF16))
                else:
                    old = stat[hh, 0:1]
                    new = jnp.maximum(old, top)
                    scale = jnp.exp(old - new)
                    p = jnp.exp(s - new)
                    stat[hh, 1:2] = stat[hh, 1:2] * scale + jnp.sum(p, axis=0, keepdims=True)
                    acc[hh] = acc[hh] * scale + dot(vals_t, p.astype(BF16))
                stat[hh, 0:1] = new

    tick()
    fold(0, z % 2 == 0)
    z_exchange(1).start()
    attend(0)
    tick(3)
    fold(1, z < 2)
    hop_start(0)
    tick(2)
    attend(1)
    hop_wait(0)
    hop_start(1)
    tick(2)
    hop_wait(1)
    hop_start(2)
    tick(2)
    attend(2)
    hop_wait(2)
    hop_start(3)
    tick(2)
    hop_wait(3)
    share_start()
    attend(3)
    attend(4)

    def partial(i):
        return accs.at[i], accr.at[i], a_s.at[i], a_r.at[i], (xn_grp if i == 2 else sib_grp), ctx

    def partial_stats(i):
        return stats.at[i], statr.at[i], t_s.at[i], t_r.at[i], (xn_grp if i == 2 else sib_grp), ctx

    for i, m in ((1, quad_member[2]), (0, quad_member[0])):
        accs[i] = acc[m].astype(BF16)
        stats[i] = stat[m]
        copy(*partial_stats(i)).start()
        copy(*partial(i)).start()

    def project(p, heads, w_ref):
        for b in range(8):
            part = dot(heads, w_ref[:, b * 256 : (b + 1) * 256]).astype(BF16)
            pbuf[p, 0, b] = part[:, :DHD]
            pbuf[p, 1, b] = part[:, DHD:]
            i = p * 8 + b
            copy(pbuf.at[p, 1 - c, b], r1.at[p, b], s1_s.at[i], s1_r.at[i], sib_grp, ctx).start()

    half = [pl.ds(0, TOK // 2), pl.ds(TOK // 2, TOK // 2)]
    step1_grp, step2_grp = [xn_grp, xm_grp], [xm_grp, xn_grp]
    step1_x, step2_x = [xn, xm], [xm, xn]

    def pair_half(p, b, a):
        return pbuf[p, c, b, half[a]].astype(F32) + r1[p, b, half[a]].astype(F32)

    def copy_x1(p, a):
        i = p * 2 + a
        return copy(s2.at[p, a], r2.at[p, a], s2_s.at[i], s2_r.at[i], step1_grp[a], ctx)

    def copy_x2(p, a):
        i = 4 + p * 2 + a
        return copy(s4.at[p, a], r4.at[p, a], s2_s.at[i], s2_r.at[i], step2_grp[a], ctx)

    def across_x1(p):
        for b in range(8):
            arrived(r1.at[p, b], s1_r.at[p * 8 + b])
        for a in range(2):
            for e in range(2):
                s2[p, a, 0, e] = pair_half(p, step1_x[a] * 2 + e, a).astype(BF16)
                s2[p, a, 1, e] = pair_half(p, xo * 2 + e, a).astype(BF16)
            copy_x1(p, a).start()

    def across_x2(p):
        for a in range(2):
            arrived(r2.at[p, a], s2_r.at[p * 2 + a])
            for e in range(2):
                s4[p, a, e] = (pair_half(p, step2_x[a] * 2 + e, a) + r2[p, a, 1, e].astype(F32)).astype(BF16)
            copy_x2(p, a).start()

    def across_z(p):
        near = []
        for a in range(2):
            arrived(r4.at[p, a], s2_r.at[4 + p * 2 + a])
            far = pair_half(p, x * 2 + 1 - zh, a) + r2[p, a, 0, 1 - zh].astype(F32) + r4[p, a, 1 - zh].astype(F32)
            s3[p, half[a]] = far.astype(BF16)
            near.append(pair_half(p, x * 2 + zh, a) + r2[p, a, 0, zh].astype(F32) + r4[p, a, zh].astype(F32))
        copy(s3.at[p], r3.at[p], s3_s.at[p], s3_r.at[p], z_grp, ctx).start()
        return jnp.concatenate(near, axis=0)

    def finish(p, near, o_ref):
        arrived(r3.at[p], s3_r.at[p])
        o_ref[...] = (near + r3[p].astype(F32)).astype(BF16)

    for load in (loads[9], loads[11]):
        load.wait()
    share_wait()
    heads = []
    for h in range(2):
        e_hi, e_lo = split(eff[h, :, :DHD])
        core = dot(e_hi, state[h], NT) + dot(e_lo, state[h], NT) + eff[h, :, DHD:]
        squares = jnp.mean(core * core, axis=1, keepdims=True)
        gate = dgate_ref[:, h * DHD : (h + 1) * DHD].astype(F32)
        normed = core * lax.rsqrt(squares + EPS) * gain_ref[...]
        heads.append((normed * gate * jax.nn.sigmoid(gate)).astype(BF16))
    def joined(accs_, stats_):
        top = stats_[0][0:1]
        for st in stats_[1:]:
            top = jnp.maximum(top, st[0:1])
        mixed, total = 0.0, 0.0
        for ac, st in zip(accs_, stats_):
            scale = jnp.exp(st[0:1] - top)
            mixed += ac.astype(F32) * scale
            total += st[1:2] * scale
        return mixed, top, total

    for i in (1, 0):
        arrived(statr.at[i], t_r.at[i])
        arrived(accr.at[i], a_r.at[i])
    for i, m in ((2, quad_member[1]), (3, member)):
        mixed, top, total = joined([acc[m], accr[3 - i]], [stat[m], statr[3 - i]])
        if i == 2:
            accs[i] = mixed.astype(BF16)
            stats[i, 0:1] = top
            stats[i, 1:2] = total
            copy(*partial_stats(i)).start()
            copy(*partial(i)).start()
        else:
            acc[m] = mixed
            stat[m, 0:1] = top
            stat[m, 1:2] = total
    project(1, jnp.concatenate(heads, axis=1), wd_ref)
    across_x1(1)
    for load in (loads[10], loads[12]):
        load.wait()
    arrived(statr.at[2], t_r.at[2])
    arrived(accr.at[2], a_r.at[2])
    mixed, _, total = joined([acc[member], accr[2]], [stat[member], statr[2]])
    core_out = (mixed / total).T
    attn_heads = (core_out * jax.nn.sigmoid(agate_ref[...].astype(F32))).astype(BF16)
    project(0, attn_heads, wa_ref)
    across_x2(1)
    across_x1(0)
    near_d = across_z(1)
    across_x2(0)
    finish(1, near_d, od_ref)
    near_a = across_z(0)
    finish(0, near_a, oa_ref)

    for i in range(3):
        copy(kv.at[0, :, z], kv.at[0, :, z], z_s.at[i], kv_r.at[z], grp, row_ctx[i]).wait_send()
        copy(qall.at[member], qall.at[member], q_s.at[i], q_r.at[i], quad_grp[i], ctx).wait_send()
        copy(*partial_stats(i)).wait_send()
        copy(*partial(i)).wait_send()
    for dy in range(4):

        @pl.when((y >= dy) & (y < 7))
        def _():
            for zs in range(4):
                forward(dy, zs).wait_send()

    for step in range(2):
        z_exchange(step).wait_send()
    for d in range(3):
        share(d).wait_send()

    @pl.when(y < 7)
    def _():
        for k in range(4):
            row_hop(k).wait_send()

    for p in range(2):
        for b in range(8):
            i = p * 8 + b
            copy(pbuf.at[p, 1 - c, b], r1.at[p, b], s1_s.at[i], s1_r.at[i], sib_grp, ctx).wait_send()
        for a in range(2):
            copy_x1(p, a).wait_send()
            copy_x2(p, a).wait_send()
        copy(s3.at[p], r3.at[p], s3_s.at[p], s3_r.at[p], z_grp, ctx).wait_send()


def local(
    queries,
    keys,
    values,
    attn_gate,
    delta_query,
    delta_key,
    delta_value,
    delta_gate,
    decay_log,
    beta,
    norm_gain,
    attn_out_weight,
    delta_out_weight,
    doc_lengths,
):
    vmem = pl.BlockSpec(memory_space=pltpu.VMEM)
    anywhere = pl.BlockSpec(memory_space=pltpu.HBM)
    dma = lambda n: pltpu.SemaphoreType.DMA((n,))
    out = jax.ShapeDtypeStruct((TOK, DHD), BF16)
    return pl.pallas_call(
        kernel,
        out_shape=(out, out),
        in_specs=[pl.BlockSpec(memory_space=pltpu.SMEM)] + [anywhere] * 13,
        out_specs=(vmem, vmem),
        scratch_shapes=[
            pltpu.VMEM((TOK, HD), BF16),
            pltpu.VMEM((TOK, HD), BF16),
            pltpu.VMEM((TOK, DHD), BF16),
            pltpu.VMEM((TOK, DHD), BF16),
            pltpu.VMEM((TOK, 2 * DHD), BF16),
            pltpu.VMEM((TOK, 2 * DHD), BF16),
            pltpu.VMEM((2, TOK), F32),
            pltpu.VMEM((2, TOK), F32),
            pltpu.VMEM((1, DHD), F32),
            pltpu.VMEM((256, 2048), BF16),
            pltpu.VMEM((256, 2048), BF16),
            pltpu.VMEM((4, TOK, HD), BF16),
            pltpu.VMEM((5, 2, 4, PIECE, HD), BF16),
            pltpu.VMEM((4, HD, TOK), F32),
            pltpu.VMEM((4, 8, TOK), F32),
            pltpu.VMEM((3, HD, TOK), BF16),
            pltpu.VMEM((3, HD, TOK), BF16),
            pltpu.VMEM((3, 8, TOK), F32),
            pltpu.VMEM((3, 8, TOK), F32),
            pltpu.VMEM((3, 2, MSG, DHD), BF16),
            pltpu.VMEM((2, 2, MSG, DHD), BF16),
            pltpu.VMEM((4, 2, QUARTER, DHD), BF16),
            pltpu.VMEM((4, 2, QUARTER, DHD), BF16),
            pltpu.VMEM((2, DHD, DHD), BF16),
            pltpu.VMEM((2, DHD, DHD), BF16),
            pltpu.VMEM((2, TOK, 2 * DHD), F32),
            pltpu.VMEM((2, 2, 8, TOK, DHD), BF16),
            pltpu.VMEM((2, 8, TOK, DHD), BF16),
            pltpu.VMEM((2, 2, 2, 2, TOK // 2, DHD), BF16),
            pltpu.VMEM((2, 2, 2, 2, TOK // 2, DHD), BF16),
            pltpu.VMEM((2, 2, 2, TOK // 2, DHD), BF16),
            pltpu.VMEM((2, 2, 2, TOK // 2, DHD), BF16),
            pltpu.VMEM((2, TOK, DHD), BF16),
            pltpu.VMEM((2, TOK, DHD), BF16),
            dma(13),
            dma(3),
            dma(3),
            dma(3),
            dma(16),
            dma(20),
            dma(2),
            dma(2),
            dma(4),
            dma(4),
            dma(3),
            dma(3),
            dma(3),
            dma(3),
            dma(3),
            dma(3),
            dma(16),
            dma(16),
            dma(8),
            dma(8),
            dma(2),
            dma(2),
        ],
        compiler_params=pltpu.CompilerParams(
            collective_id=0, has_side_effects=True, vmem_limit_bytes=64 * 1024 * 1024
        ),
        cost_estimate=pl.CostEstimate(flops=4 * 10**9, bytes_accessed=6 * 10**6, transcendentals=2 * 10**6),
    )(
        doc_lengths,
        queries,
        keys,
        values,
        attn_gate,
        delta_query,
        delta_key,
        delta_value,
        delta_gate,
        decay_log,
        beta,
        norm_gain.reshape(1, DHD),
        attn_out_weight,
        delta_out_weight,
    )


def solution(mesh):
    placed = (
        P("ctx", "grp"),
        P("ctx", None),
        P("ctx", None),
        P("ctx", "grp"),
        P("ctx", "grp"),
        P("ctx", "grp"),
        P("ctx", "grp"),
        P("ctx", "grp"),
        P("grp", "ctx"),
        P("grp", "ctx"),
        P(),
        P("grp", None),
        P("grp", None),
        P(),
    )
    return jax.shard_map(
        local,
        mesh=mesh,
        in_specs=placed,
        out_specs=(P("ctx", "grp"), P("ctx", "grp")),
        check_vma=False,
    )
```
